128 devices in a mesh: seq: 8 (over x, core), exp: 16 (over z, y).
Axes of the slice: x: 4, y: 4, z: 4, core: 2. Of those that a mesh axis runs over, the one named last changes fastest.
Arguments:
- queries: bfloat16 [16, 1024, 4096], P('exp', 'seq'), may hold values from -6 to 6
- keys: bfloat16 [16, 1024, 4096], P('exp', 'seq'), may hold values from -6 to 6
- values: bfloat16 [16, 1024, 4096], P('exp', 'seq'), may hold values from -6 to 6
- residual_in: bfloat16 [16, 1024, 4096], P('exp', 'seq'), may hold values from -6 to 6
- cached_moe: bfloat16 [16, 1024, 4096], P('exp', 'seq'), may hold values from -6 to 6
- norm_gain: bfloat16 [4096], replicated, may hold values from 0.25 to 1.75
- still_masked: int32 [16, 1024], P('exp', 'seq'), may hold values from 0 to 1, as said below
- expert_ids: int32 [16, 1024, 8], P('exp', 'seq'), may hold values from 0 to 63, as said below
- gate_weights: float32 [16, 1024, 8], P('exp', 'seq'), may hold values from 0.05 to 1
- w_gate: bfloat16 [128, 4096, 768], P(('seq', 'exp')), may hold values from -0.09375 to 0.09375
- w_up: bfloat16 [128, 4096, 768], P(('seq', 'exp')), may hold values from -0.09375 to 0.09375
- w_down: bfloat16 [128, 768, 4096], P(('seq', 'exp')), may hold values from -0.15625 to 0.15625
Outputs:
- layer_out: bfloat16 [16, 1024, 4096], P('exp', 'seq')
The draws below stay inside these ranges and needn't reach their ends.
Inputs may be any that keep to these rules, and one draw needn't show every extreme that they name: `still_masked`: among the 128 rows that one device holds at most 48 are still masked and at least half of that; some device has exactly 48. `expert_ids`: each row names 8 different experts. Among the still-masked rows of one device no expert is named more than 8 times, and on every device some expert is named exactly 8 times.
All inputs are finite; a program needn't handle non-finite values.
Results may differ from the reference program's by a relative error of at most 0.011.
Values may be sent and summed in bfloat16 or wider, within the bound.
No kernel may reach another device: no remote copies, remote signals or barrier semaphores. Data moves between devices by JAX's collectives and lax.ppermute only.
A program may use at most 192 MiB of HBM per device.

```python
import math
import jax
import jax.numpy as jnp
from jax import lax

D = 4096
HEAD_DIM = 128
HEADS = 32
FF = 1536
HALF = 768
TOP = 8
TOK_DEV = 128
SEQ_LEN = 1024
SEQS = 16
EXPERTS = 64
MASK_MOST = 48
MOST = 8
DEVICES = 128


def masked_layout(key):
    blocks = SEQS * (SEQ_LEN // TOK_DEV)
    key_count, key_top, key_perm = jax.random.split(jax.random.fold_in(key, 101), 3)
    counts = jax.random.randint(key_count, (blocks,), MASK_MOST // 2, MASK_MOST + 1)
    chosen = jax.random.randint(key_top, (), 0, blocks)
    counts = jnp.where(jnp.arange(blocks) == chosen, MASK_MOST, counts)
    ranks = jax.vmap(lambda single: jax.random.permutation(single, TOK_DEV))(jax.random.split(key_perm, blocks))
    return (ranks < counts[:, None]).astype(jnp.int32)


def draw_still_masked(key, part):
    row_flags = masked_layout(key)
    return row_flags.reshape(SEQS, SEQ_LEN)


def draw_expert_ids(key, part):
    row_flags = masked_layout(key)
    key = jax.random.fold_in(key, 2)
    blocks = SEQS * (SEQ_LEN // TOK_DEV)
    groups = EXPERTS // TOP
    key_order, key_first, key_second, key_spare = jax.random.split(key, 4)
    order = jax.random.permutation(key_order, EXPERTS)
    first_group = jnp.minimum(jax.random.randint(key_first, (blocks,), 0, groups), jax.random.randint(key_second, (blocks,), 0, groups))
    rank = jnp.cumsum(row_flags, axis=1) - 1
    spare = jax.random.randint(key_spare, (blocks, TOK_DEV), 0, groups)
    group = jnp.where(row_flags == 1, (first_group[:, None] + rank // MOST) % groups, spare)
    chosen = order[group[..., None] * TOP + jnp.arange(TOP)[None, None, :]]
    return chosen.reshape(SEQS, SEQ_LEN, TOP).astype(jnp.int32)


def draw_queries(key, part):
    key = jax.random.fold_in(key, 3)
    shape = (SEQS, SEQ_LEN, D)
    return jax.random.normal(key, shape).astype(jnp.bfloat16)


def draw_keys(key, part):
    key = jax.random.fold_in(key, 4)
    shape = (SEQS, SEQ_LEN, D)
    return jax.random.normal(key, shape).astype(jnp.bfloat16)


def steps_of(stream_key, dims, pieces, least, top_value):
    level, own = 1.0, jax.random.fold_in(stream_key, 6)
    for dim, blocks in pieces:
        heights = jnp.exp(jax.random.uniform(jax.random.fold_in(own, dim), (blocks,), jnp.float32, least / len(pieces), top_value / len(pieces)))
        level = level * jnp.repeat(heights, dims[dim] // blocks).reshape([-1 if axis == dim else 1 for axis in range(len(dims))])
    return level


def centred(rng, dims, spread, most, cuts=(), kind=jnp.bfloat16):
    drawn = jax.random.normal(rng, dims, jnp.float32) * spread
    if len(cuts) > 0:
        drawn = steps_of(rng, dims, cuts, -0.22, 0.18) * drawn
    return jnp.clip(drawn, min=-most, max=most).astype(kind)


def setup_inputs(seed: int = 0) -> dict:
    key_of = jax.random.split(jax.random.key(seed), 13)
    return {
        "queries": draw_queries(jax.random.fold_in(key_of[12], 71), 0),
        "keys": draw_keys(jax.random.fold_in(key_of[12], 71), 0),
        "values": centred(key_of[2], (SEQS, SEQ_LEN, D), 1.0, 6.0, ((0, 16), (1, 8))),
        "residual_in": centred(key_of[3], (SEQS, SEQ_LEN, D), 1.0, 6.0, ((0, 16), (1, 8))),
        "cached_moe": centred(key_of[4], (SEQS, SEQ_LEN, D), 1.0, 6.0, ((0, 16), (1, 8))),
        "norm_gain": jnp.clip(1.0 + 0.15 * jax.random.normal(key_of[5], (D,), jnp.float32), 0.25, 1.75).astype(jnp.bfloat16),
        "still_masked": draw_still_masked(jax.random.fold_in(key_of[12], 71), 0),
        "expert_ids": draw_expert_ids(jax.random.fold_in(key_of[12], 71), 0),
        "gate_weights": jnp.clip(jnp.exp(math.log(1.0) - 2.9957323 * jax.random.uniform(key_of[8], (SEQS, SEQ_LEN, TOP), jnp.float32) ** steps_of(key_of[8], (SEQS, SEQ_LEN, TOP), ((0, 16), (1, 8)), -0.2, 0.2)), 0.05, 1.0),
        "w_gate": centred(key_of[9], (DEVICES, D, HALF), D ** -0.5, 0.09375, ((0, 128),)),
        "w_up": centred(key_of[10], (DEVICES, D, HALF), D ** -0.5, 0.09375, ((0, 128),)),
        "w_down": centred(key_of[11], (DEVICES, HALF, D), FF ** -0.5, 0.15625, ((0, 128),)),
    }


def attend(query_rows, key_rows, value_rows):
    length = query_rows.shape[0]
    q_heads = query_rows.astype(jnp.float32).reshape(length, HEADS, HEAD_DIM)
    k_heads = key_rows.astype(jnp.float32).reshape(length, HEADS, HEAD_DIM)
    v_heads = value_rows.astype(jnp.float32).reshape(length, HEADS, HEAD_DIM)
    scores = jnp.einsum('qhd,khd->hqk', q_heads, k_heads) / jnp.sqrt(jnp.float32(HEAD_DIM))
    peak = lax.optimization_barrier(jnp.max(scores, axis=-1, keepdims=True))
    expo = jnp.exp(scores - peak)
    probs = (expo / lax.optimization_barrier(jnp.sum(expo, axis=-1, keepdims=True))).astype(jnp.bfloat16)
    mixed = jnp.einsum('hqk,khd->qhd', probs.astype(jnp.float32), v_heads)
    return mixed.reshape(length, D).astype(jnp.bfloat16)

def reference(queries, keys, values, residual_in, cached_moe, norm_gain, still_masked, expert_ids, gate_weights, w_gate, w_up, w_down):
    attn = lax.map(lambda trio: attend(trio[0], trio[1], trio[2]), (queries, keys, values))
    hidden = residual_in.astype(jnp.float32) + attn.astype(jnp.float32)
    meansq = lax.optimization_barrier(jnp.mean(hidden * hidden, axis=-1, keepdims=True))
    normed = (hidden * lax.rsqrt(meansq + 1e-06) * norm_gain.astype(jnp.float32)).astype(jnp.bfloat16)
    total_rows = SEQS * SEQ_LEN
    flat_normed = normed.reshape(total_rows, D)
    flat_flags = still_masked.reshape(total_rows)
    flat_ids = expert_ids.reshape(total_rows, TOP)
    flat_gates = gate_weights.reshape(total_rows, TOP).astype(jnp.float32)
    capacity = DEVICES * MOST
    slot_range = jnp.arange(capacity, dtype=jnp.int32)

    def expert_step(summed, expert):
        hits = (flat_ids == expert) & (flat_flags[:, None] == 1)
        coef = lax.optimization_barrier(jnp.sum(jnp.where(hits, flat_gates, jnp.float32(0.0)), axis=-1))
        named = jnp.any(hits, axis=-1)
        picked = jnp.nonzero(named, size=capacity, fill_value=0)[0].astype(jnp.int32)
        count = jnp.sum(named.astype(jnp.int32))
        row_coef = jnp.where(slot_range < count, coef[picked], jnp.float32(0.0))
        rows = flat_normed[picked]
        both = jnp.zeros((capacity, D), jnp.float32)
        for half_index in range(2):
            entry = 2 * expert + half_index
            gate_part = jnp.dot(rows, w_gate[entry], preferred_element_type=jnp.float32)
            up_part = jnp.dot(rows, w_up[entry], preferred_element_type=jnp.float32)
            act = (jax.nn.silu(gate_part) * up_part).astype(jnp.bfloat16)
            part = jnp.dot(act, w_down[entry], preferred_element_type=jnp.float32).astype(jnp.bfloat16)
            both = both + part.astype(jnp.float32)
        summed = summed.at[picked].add(both * row_coef[:, None])
        return (summed, None)
    start_sum = jnp.zeros((total_rows, D), jnp.float32)
    summed, _ = lax.scan(expert_step, start_sum, jnp.arange(EXPERTS, dtype=jnp.int32))
    moe = jnp.where(flat_flags[:, None] == 1, summed, cached_moe.reshape(total_rows, D).astype(jnp.float32))
    layer_out = (hidden.reshape(total_rows, D) + moe).astype(jnp.bfloat16)
    return layer_out.reshape(SEQS, SEQ_LEN, D)
```

```python
import functools
import math

import jax
import jax.numpy as jnp
from jax import lax
from jax.experimental import pallas as pl
from jax.experimental.pallas import tpu as pltpu
from jax.sharding import PartitionSpec as P

HEAD_DIM = 128
TOP = 8
SLOTS = 8
bf16 = jnp.bfloat16
f32 = jnp.float32


def params(mib, *semantics):
    return pltpu.CompilerParams(
        vmem_limit_bytes=mib * 1024 * 1024, dimension_semantics=semantics or None
    )


def attend_kernel(qkv_ref, out_ref):
    blocks, _, rows, _ = qkv_ref.shape
    length = blocks * rows
    scale = math.log2(math.e) / math.sqrt(HEAD_DIM)
    k_all = qkv_ref[:, 1].reshape(length, HEAD_DIM)
    v_all = qkv_ref[:, 2].reshape(length, HEAD_DIM)
    step = 2
    for first in range(0, blocks, step):
        q_part = qkv_ref[first : first + step, 0].reshape(step * rows, HEAD_DIM)
        scores = lax.dot_general(
            q_part, k_all, (((1,), (1,)), ((), ())), preferred_element_type=f32
        )
        peak = jnp.max(scores, axis=-1, keepdims=True)
        expo = jnp.exp2((scores - peak) * scale)
        total = jnp.sum(expo, axis=-1, keepdims=True)
        mixed = jnp.dot(expo.astype(bf16), v_all, preferred_element_type=f32)
        out_ref[first : first + step] = (
            (mixed / total).astype(bf16).reshape(step, rows, HEAD_DIM)
        )


def attend(qkv):
    blocks, three, rows, cols = qkv.shape
    heads = cols // HEAD_DIM
    return pl.pallas_call(
        attend_kernel,
        grid=(heads,),
        in_specs=[pl.BlockSpec((blocks, three, rows, HEAD_DIM), lambda h: (0, 0, 0, h))],
        out_specs=pl.BlockSpec((blocks, rows, HEAD_DIM), lambda h: (0, 0, h)),
        out_shape=jax.ShapeDtypeStruct((blocks, rows, cols), bf16),
        compiler_params=params(40),
        name="attend",
    )(qkv)


def dispatch_kernel(attn_ref, res_ref, gain_ref, pick_ref, out_ref, rs_ref):
    step = pl.program_id(0)
    groups, rows, cols = attn_ref.shape

    @pl.when(step == 0)
    def _():
        total = jnp.zeros((rows, 1), f32)
        for g in range(groups):
            hid = res_ref[:, g * cols : (g + 1) * cols].astype(f32) + attn_ref[g].astype(f32)
            total += jnp.sum(hid * hid, axis=-1, keepdims=True)
        rs_ref[...] = lax.rsqrt(total / (groups * cols) + 1e-06)

    here = pl.ds(pl.multiple_of(step * cols, cols), cols)
    hid = res_ref[:, here].astype(f32) + attn_ref[step].astype(f32)
    normed = (hid * rs_ref[...] * gain_ref[:, here].astype(f32)).astype(bf16)
    picked = jnp.dot(pick_ref[...], normed, preferred_element_type=f32)
    experts = out_ref.shape[0]
    picked = picked.reshape(experts, SLOTS, cols).astype(bf16)
    out_ref[:, 0] = picked
    out_ref[:, 1] = picked


def dispatch(attn, residual, gain, pick):
    groups, rows, cols = attn.shape
    experts = pick.shape[0] // SLOTS
    width = groups * cols
    return pl.pallas_call(
        dispatch_kernel,
        grid=(groups,),
        in_specs=[
            pl.BlockSpec((groups, rows, cols), lambda j: (0, 0, 0)),
            pl.BlockSpec((rows, width), lambda j: (0, 0)),
            pl.BlockSpec((1, width), lambda j: (0, 0)),
            pl.BlockSpec(pick.shape, lambda j: (0, 0)),
        ],
        out_specs=pl.BlockSpec((experts, 2, SLOTS, cols), lambda j: (0, 0, 0, j)),
        out_shape=jax.ShapeDtypeStruct((experts, 2, SLOTS, width), bf16),
        scratch_shapes=[pltpu.VMEM((rows, 1), f32)],
        compiler_params=params(40),
        name="dispatch",
    )(attn, residual, gain, pick)


def expert_kernel(rows_ref, gate_ref, up_ref, down_ref, out_ref):
    tile = rows_ref[...]
    gate_part = jnp.dot(tile, gate_ref[...], preferred_element_type=f32)
    up_part = jnp.dot(tile, up_ref[...], preferred_element_type=f32)
    act = (gate_part / (1.0 + jnp.exp(-gate_part)) * up_part).astype(bf16)
    out_ref[...] = jnp.dot(act, down_ref[...], preferred_element_type=f32).astype(bf16)


def expert(rows, gate, up, down):
    total, width = rows.shape
    half = gate.shape[1]
    tile = 256
    return pl.pallas_call(
        expert_kernel,
        grid=(total // tile,),
        in_specs=[
            pl.BlockSpec((tile, width), lambda i: (i, 0)),
            pl.BlockSpec((width, half), lambda i: (0, 0)),
            pl.BlockSpec((width, half), lambda i: (0, 0)),
            pl.BlockSpec((half, width), lambda i: (0, 0)),
        ],
        out_specs=pl.BlockSpec((tile, width), lambda i: (i, 0)),
        out_shape=jax.ShapeDtypeStruct((total, width), bf16),
        compiler_params=params(60),
        name="expert",
    )(rows, gate, up, down)


def combine_kernel(back_ref, mix_ref, attn_ref, res_ref, cached_ref, flag_ref, out_ref):
    rows = res_ref.shape[0]
    both = jnp.dot(mix_ref[...], back_ref[...], preferred_element_type=f32)
    mixed = both[:rows] + both[rows:]
    moe = jnp.where(flag_ref[...] == 1, mixed, cached_ref[...].astype(f32))
    hid = res_ref[...].astype(f32) + attn_ref[0].astype(f32)
    out_ref[...] = (hid + moe).astype(bf16)


def combine(back, mix, attn, residual, cached, flags):
    groups, rows, cols = attn.shape
    slots, width = back.shape
    return pl.pallas_call(
        combine_kernel,
        grid=(groups,),
        in_specs=[
            pl.BlockSpec((slots, cols), lambda j: (0, j)),
            pl.BlockSpec(mix.shape, lambda j: (0, 0)),
            pl.BlockSpec((1, rows, cols), lambda j: (j, 0, 0)),
            pl.BlockSpec((rows, cols), lambda j: (0, j)),
            pl.BlockSpec((rows, cols), lambda j: (0, j)),
            pl.BlockSpec((rows, 1), lambda j: (0, 0)),
        ],
        out_specs=pl.BlockSpec((rows, cols), lambda j: (0, j)),
        out_shape=jax.ShapeDtypeStruct((rows, width), bf16),
        compiler_params=params(40),
        name="combine",
    )(back, mix, attn, residual, cached, flags)


def per_device(
    queries,
    keys,
    values,
    residual_in,
    cached_moe,
    norm_gain,
    still_masked,
    expert_ids,
    gate_weights,
    w_gate,
    w_up,
    w_down,
):
    rows, width = queries.shape[1:]
    seq_count = lax.axis_size("seq")
    devices = seq_count * lax.axis_size("exp")
    experts = devices // 2
    cols = width // seq_count

    qkv = jnp.stack([queries[0], keys[0], values[0]])
    qkv = qkv.reshape(3, rows, seq_count, cols).transpose(2, 0, 1, 3)
    qkv = lax.all_to_all(qkv, "seq", split_axis=0, concat_axis=0, tiled=True)

    flags = still_masked[0][:, None]
    hits = (expert_ids[0][:, :, None] == jnp.arange(experts, dtype=jnp.int32)) & (
        flags[:, :, None] == 1
    )
    named = jnp.any(hits, axis=1)
    gates = jnp.sum(jnp.where(hits, gate_weights[0][:, :, None], 0.0), axis=1)
    below = jnp.tril(jnp.ones((rows, rows), bf16), -1)
    before = jnp.dot(below, named.astype(bf16), preferred_element_type=f32).astype(jnp.int32)
    slot = jnp.where(named, before, -1)
    pick = (slot.T[:, None, :] == jnp.arange(SLOTS)[None, :, None]).astype(bf16)
    pick = pick.reshape(experts * SLOTS, rows)
    spread = jnp.where(
        slot[:, :, None, None] == jnp.arange(SLOTS)[None, None, None, :],
        gates[:, :, None, None],
        0.0,
    )
    spread = jnp.broadcast_to(spread, (rows, experts, 2, SLOTS)).reshape(rows, devices * SLOTS)
    high = spread.astype(bf16)
    low = (spread - high.astype(f32)).astype(bf16)
    mix = jnp.concatenate([high, low], axis=0)

    attn = attend(qkv)
    attn = lax.all_to_all(attn, "seq", split_axis=0, concat_axis=0, tiled=True)
    outgoing = dispatch(attn, residual_in[0], norm_gain[None, :], pick)
    arrived = lax.all_to_all(
        outgoing.reshape(devices, SLOTS, width),
        ("seq", "exp"),
        split_axis=0,
        concat_axis=0,
        tiled=True,
    )
    done = expert(arrived.reshape(devices * SLOTS, width), w_gate[0], w_up[0], w_down[0])
    back = lax.all_to_all(
        done.reshape(devices, SLOTS, width),
        ("seq", "exp"),
        split_axis=0,
        concat_axis=0,
        tiled=True,
    )
    out = combine(
        back.reshape(devices * SLOTS, width), mix, attn, residual_in[0], cached_moe[0], flags
    )
    return out[None]


def solution(mesh):
    return jax.shard_map(
        per_device,
        mesh=mesh,
        in_specs=(
            P("exp", "seq", None),
            P("exp", "seq", None),
            P("exp", "seq", None),
            P("exp", "seq", None),
            P("exp", "seq", None),
            P(),
            P("exp", "seq"),
            P("exp", "seq", None),
            P("exp", "seq", None),
            P(("seq", "exp"), None, None),
            P(("seq", "exp"), None, None),
            P(("seq", "exp"), None, None),
        ),
        out_specs=P("exp", "seq", None),
        check_vma=False,
    )
```

```python
import math

import jax
import jax.numpy as jnp
from jax import lax
from jax.experimental import pallas as pl
from jax.experimental.pallas import tpu as pltpu
from jax.sharding import PartitionSpec as P

HEAD_DIM = 128
TOP = 8
SLOTS = 8
bf16 = jnp.bfloat16
f32 = jnp.float32


def params(mib):
    return pltpu.CompilerParams(vmem_limit_bytes=mib * 1024 * 1024)


def iota(shape, dim):
    return lax.broadcasted_iota(jnp.int32, shape, dim)


def ones(where):
    return jnp.where(where, jnp.float32(1.0), jnp.float32(0.0)).astype(bf16)


def dot(a, b, dims=((1,), (0,))):
    return lax.dot_general(a, b, (dims, ((), ())), preferred_element_type=f32)


def prepare_kernel(
    q_ref, k_ref, v_ref, res_ref, flag_ref, ids_ref, gates_ref, out_ref, meta_ref, own_ref, pick_ref
):
    rows = q_ref.shape[0]
    most = pick_ref.shape[0]

    @pl.when(pl.program_id(0) == 0)
    def _():
        experts = own_ref.shape[2]
        flags = ones(jnp.broadcast_to(flag_ref[...], (rows, rows)) == 1)
        upper = ones(iota((rows, rows), 0) < iota((rows, rows), 1))
        lower = ones(iota((rows, rows), 0) > iota((rows, rows), 1))
        eye = ones(iota((rows, rows), 0) == iota((rows, rows), 1))
        rank = dot(flags, upper)[:1].astype(jnp.int32)
        pick = ones((iota((most, rows), 0) == rank) & (flag_ref[...] == 1))
        pick_ref[...] = pick
        masked = dot(eye, flags, ((1,), (1,)))[:, :1] > 0.5
        named = jnp.zeros((rows, experts), f32)
        gates = jnp.zeros((rows, experts), f32)
        for k in range(TOP):
            hit = (ids_ref[:, k : k + 1] == iota((rows, experts), 1)) & masked
            named = jnp.where(hit, 1.0, named)
            gates = jnp.where(hit, gates_ref[:, k : k + 1], gates)
        place = named * (dot(lower, named.astype(bf16)) + 1.0)
        place = place.astype(bf16)
        high = gates.astype(bf16)
        own_ref[0] = place
        own_ref[1] = high
        own_ref[2] = (gates - high.astype(f32)).astype(bf16)
        meta_ref[...] = jnp.zeros_like(meta_ref)
        meta_ref[:experts, :most] = dot(place, pick, ((0,), (1,))).astype(bf16)
        meta_ref[experts:] = pick

    out_ref[0, :rows] = q_ref[...]
    out_ref[0, rows : 2 * rows] = k_ref[...]
    out_ref[0, 2 * rows : 3 * rows] = v_ref[...]
    out_ref[0, 3 * rows :] = dot(pick_ref[...], res_ref[...]).astype(bf16)


def prepare(q, k, v, res, flags, ids, gates, groups, experts, most):
    rows, width = q.shape
    cols = width // groups
    piece = pl.BlockSpec((rows, cols), lambda j: (0, j))
    return pl.pallas_call(
        prepare_kernel,
        grid=(groups,),
        in_specs=[
            piece,
            piece,
            piece,
            piece,
            pl.BlockSpec((1, rows), lambda j: (0, 0)),
            pl.BlockSpec((rows, TOP), lambda j: (0, 0)),
            pl.BlockSpec((rows, TOP), lambda j: (0, 0)),
        ],
        out_specs=[
            pl.BlockSpec((1, 3 * rows + most, cols), lambda j: (j, 0, 0)),
            pl.BlockSpec((experts + most, rows), lambda j: (0, 0)),
            pl.BlockSpec((3, rows, experts), lambda j: (0, 0, 0)),
        ],
        out_shape=[
            jax.ShapeDtypeStruct((groups, 3 * rows + most, cols), bf16),
            jax.ShapeDtypeStruct((experts + most, rows), bf16),
            jax.ShapeDtypeStruct((3, rows, experts), bf16),
        ],
        scratch_shapes=[pltpu.VMEM((most, rows), bf16)],
        compiler_params=params(24),
        name="prepare",
    )(q, k, v, res, flags, ids, gates)


def attend_kernel(in_ref, meta_ref, gain_ref, attn_ref, out_ref, place_ref):
    blocks, rows, _ = attn_ref.shape
    experts = out_ref.shape[0]
    most = in_ref.shape[1] - 3 * rows
    length = blocks * rows

    @pl.when(pl.program_id(0) == 0)
    def _():
        for b in range(blocks):
            table = meta_ref[b, :experts, :most].astype(f32)
            wanted = iota((experts, SLOTS, most), 1).astype(f32) + 1.0
            hit = jnp.where(table[:, None, :] == wanted, 1.0, 0.0)
            place_ref[b] = hit.reshape(experts * SLOTS, most).astype(bf16)

    scale = math.log2(math.e) / math.sqrt(HEAD_DIM)
    k_all = in_ref[:, rows : 2 * rows].reshape(length, HEAD_DIM)
    v_all = in_ref[:, 2 * rows : 3 * rows].reshape(length, HEAD_DIM)
    gain = gain_ref[...].astype(f32)
    step = 2
    for first in range(0, blocks, step):
        q_part = in_ref[first : first + step, :rows].reshape(step * rows, HEAD_DIM)
        scores = dot(q_part, k_all, ((1,), (1,)))
        peak = jnp.max(scores, axis=-1, keepdims=True)
        expo = jnp.exp2((scores - peak) * scale)
        total = jnp.sum(expo, axis=-1, keepdims=True)
        mixed = dot(expo.astype(bf16), v_all)
        attn = (mixed / total).astype(bf16).reshape(step, rows, HEAD_DIM)
        attn_ref[first : first + step] = attn
        for i in range(step):
            b = first + i
            hidden = dot(meta_ref[b, experts:], attn[i]) + in_ref[b, 3 * rows :].astype(f32)
            sent = dot(place_ref[b], (hidden * gain).astype(bf16))
            sent = sent.reshape(experts, SLOTS, HEAD_DIM).astype(bf16)
            out_ref[:, 0, b] = sent
            out_ref[:, 1, b] = sent


def attend(pieces, meta, gain, rows, experts):
    blocks, total, cols = pieces.shape
    most = total - 3 * rows
    return pl.pallas_call(
        attend_kernel,
        grid=(cols // HEAD_DIM,),
        in_specs=[
            pl.BlockSpec((blocks, total, HEAD_DIM), lambda h: (0, 0, h)),
            pl.BlockSpec(meta.shape, lambda h: (0, 0, 0)),
            pl.BlockSpec((1, HEAD_DIM), lambda h: (0, h)),
        ],
        out_specs=[
            pl.BlockSpec((blocks, rows, HEAD_DIM), lambda h: (0, 0, h)),
            pl.BlockSpec((experts, 2, blocks, SLOTS, HEAD_DIM), lambda h: (0, 0, 0, 0, h)),
        ],
        out_shape=[
            jax.ShapeDtypeStruct((blocks, rows, cols), bf16),
            jax.ShapeDtypeStruct((experts, 2, blocks, SLOTS, cols), bf16),
        ],
        scratch_shapes=[pltpu.VMEM((blocks, experts * SLOTS, most), bf16)],
        compiler_params=params(40),
        name="attend",
    )(pieces, meta, gain)


CHUNKS = 4


def expert_kernel(
    rows_ref, back_ref, gate_hbm, up_hbm, down_hbm, out_ref, x_ref, gate_ref, up_ref, down_ref, sems
):
    step = pl.program_id(0)
    groups, part, per, cols = rows_ref.shape
    tile = part * per
    width, half = gate_ref.shape
    depth = width // CHUNKS

    def loads(c):
        here = pl.ds(c * depth, depth)
        return (
            pltpu.make_async_copy(gate_hbm.at[here], gate_ref.at[here], sems.at[0, c]),
            pltpu.make_async_copy(up_hbm.at[here], up_ref.at[here], sems.at[1, c]),
        )

    down_load = pltpu.make_async_copy(down_hbm, down_ref, sems.at[2, 0])

    @pl.when(step == 0)
    def _():
        for c in range(CHUNKS):
            for load in loads(c):
                load.start()
        down_load.start()

    square = jnp.zeros((tile, 1), f32)
    for g in range(groups):
        piece = rows_ref[g].reshape(tile, cols)
        x_ref[:, g * cols : (g + 1) * cols] = piece
        hidden = piece.astype(f32) * back_ref[:, g * cols : (g + 1) * cols]
        square += jnp.sum(hidden * hidden, axis=-1, keepdims=True)
    scale = lax.rsqrt(square / width + 1e-06)

    def finish(gate_part, up_part):
        gate_part = gate_part * scale
        act = (gate_part / (1.0 + jnp.exp(-gate_part)) * (up_part * scale)).astype(bf16)

        @pl.when(step == 0)
        def _():
            down_load.wait()

        span = 1024
        for c in range(0, width, span):
            result = dot(act, down_ref[:, c : c + span])
            result = result.reshape(part, groups, SLOTS, span).astype(bf16)
            for i in range(part):
                out_ref[:, i, :, c : c + span] = result[i]

    @pl.when(step == 0)
    def _():
        gate_part = jnp.zeros((tile, half), f32)
        up_part = jnp.zeros((tile, half), f32)
        for c in range(CHUNKS):
            for load in loads(c):
                load.wait()
            here = slice(c * depth, (c + 1) * depth)
            gate_part += dot(x_ref[:, here], gate_ref[here])
            up_part += dot(x_ref[:, here], up_ref[here])
        finish(gate_part, up_part)

    @pl.when(step > 0)
    def _():
        finish(dot(x_ref[...], gate_ref[...]), dot(x_ref[...], up_ref[...]))


def expert(arrived, back_gain, gate, up, down):
    groups, count, per, cols = arrived.shape
    width, half = gate.shape
    part = 256 // per
    total = count * per
    return pl.pallas_call(
        expert_kernel,
        grid=(count // part,),
        in_specs=[
            pl.BlockSpec((groups, part, per, cols), lambda i: (0, i, 0, 0)),
            pl.BlockSpec((1, width), lambda i: (0, 0)),
            pl.BlockSpec(memory_space=pl.ANY),
            pl.BlockSpec(memory_space=pl.ANY),
            pl.BlockSpec(memory_space=pl.ANY),
        ],
        out_specs=pl.BlockSpec((groups, part, SLOTS, width), lambda i: (0, i, 0, 0)),
        out_shape=jax.ShapeDtypeStruct((groups, count, SLOTS, width), bf16),
        scratch_shapes=[
            pltpu.VMEM((part * per, width), bf16),
            pltpu.VMEM((width, half), bf16),
            pltpu.VMEM((width, half), bf16),
            pltpu.VMEM((half, width), bf16),
            pltpu.SemaphoreType.DMA((3, CHUNKS)),
        ],
        compiler_params=params(50),
        cost_estimate=pl.CostEstimate(
            flops=6 * total * width * half,
            bytes_accessed=2 * (3 * width * half + 2 * total * width),
            transcendentals=total * half,
        ),
        name="expert",
    )(arrived, back_gain, gate, up, down)


def combine_kernel(back_ref, own_ref, attn_ref, res_ref, cached_ref, flag_ref, out_ref, mix_ref):
    rows, experts = own_ref.shape[1:]
    slots = back_ref.shape[0]
    per = slots // experts

    @pl.when(pl.program_id(0) == 0)
    def _():
        column = iota((experts, slots), 1)
        spread = ones(iota((experts, slots), 0) == column // per)
        wanted = (iota((rows, slots), 1) % SLOTS + 1).astype(f32)
        hit = dot(own_ref[0], spread) == wanted
        mix_ref[:rows] = jnp.where(hit, dot(own_ref[1], spread), 0.0).astype(bf16)
        mix_ref[rows:] = jnp.where(hit, dot(own_ref[2], spread), 0.0).astype(bf16)

    both = dot(mix_ref[...], back_ref[...])
    mixed = both[:rows] + both[rows:]
    moe = jnp.where(flag_ref[...] == 1, mixed, cached_ref[...].astype(f32))
    hid = res_ref[...].astype(f32) + attn_ref[0].astype(f32)
    out_ref[...] = (hid + moe).astype(bf16)


def combine(back, own, attn, residual, cached, flags):
    groups, rows, cols = attn.shape
    slots, width = back.shape
    return pl.pallas_call(
        combine_kernel,
        grid=(groups,),
        in_specs=[
            pl.BlockSpec((slots, cols), lambda j: (0, j)),
            pl.BlockSpec(own.shape, lambda j: (0, 0, 0)),
            pl.BlockSpec((1, rows, cols), lambda j: (j, 0, 0)),
            pl.BlockSpec((rows, cols), lambda j: (0, j)),
            pl.BlockSpec((rows, cols), lambda j: (0, j)),
            pl.BlockSpec((rows, 1), lambda j: (0, 0)),
        ],
        out_specs=pl.BlockSpec((rows, cols), lambda j: (0, j)),
        out_shape=jax.ShapeDtypeStruct((rows, width), bf16),
        scratch_shapes=[pltpu.VMEM((2 * rows, slots), bf16)],
        compiler_params=params(40),
        name="combine",
    )(back, own, attn, residual, cached, flags)


def exchange(blocks, axes):
    return lax.all_to_all(blocks, axes, split_axis=0, concat_axis=0, tiled=True)


def per_device(
    queries,
    keys,
    values,
    residual_in,
    cached_moe,
    norm_gain,
    still_masked,
    expert_ids,
    gate_weights,
    w_gate,
    w_up,
    w_down,
):
    rows, width = queries.shape[1:]
    seq_count = lax.axis_size("seq")
    exp_count = lax.axis_size("exp")
    devices = seq_count * exp_count
    experts = devices // 2
    cols = width // seq_count
    most = rows * 3 // 8

    pieces, meta, own = prepare(
        queries[0],
        keys[0],
        values[0],
        residual_in[0],
        still_masked,
        expert_ids[0],
        gate_weights[0],
        seq_count,
        experts,
        most,
    )
    meta = lax.all_gather(meta, "seq", axis=0)
    pieces = exchange(pieces, "seq")
    gain = norm_gain[None, :]
    own_gain = lax.dynamic_slice_in_dim(gain, lax.axis_index("seq") * cols, cols, 1)
    back_gain = 1.0 / gain.astype(f32)

    attn, outgoing = attend(pieces, meta, own_gain, rows, experts)
    arrived = exchange(outgoing.reshape(devices, seq_count * SLOTS, cols), ("seq", "exp"))
    attn, arrived = lax.optimization_barrier((attn, arrived))
    attn = exchange(attn, "seq")
    arrived = arrived.reshape(seq_count, exp_count, seq_count * SLOTS, cols)
    done = expert(arrived, back_gain, w_gate[0], w_up[0], w_down[0])
    back = exchange(done.reshape(devices, SLOTS, width), ("seq", "exp"))
    out = combine(
        back.reshape(devices * SLOTS, width),
        own,
        attn,
        residual_in[0],
        cached_moe[0],
        still_masked[0][:, None],
    )
    return out[None]


def solution(mesh):
    return jax.shard_map(
        per_device,
        mesh=mesh,
        in_specs=(
            P("exp", "seq", None),
            P("exp", "seq", None),
            P("exp", "seq", None),
            P("exp", "seq", None),
            P("exp", "seq", None),
            P(),
            P("exp", "seq"),
            P("exp", "seq", None),
            P("exp", "seq", None),
            P(("seq", "exp"), None, None),
            P(("seq", "exp"), None, None),
            P(("seq", "exp"), None, None),
        ),
        out_specs=P("exp", "seq", None),
        check_vma=False,
    )
```

```python
import math

import jax
import jax.numpy as jnp
from jax import lax
from jax.experimental import pallas as pl
from jax.experimental.pallas import tpu as pltpu
from jax.sharding import PartitionSpec as P

HEAD_DIM = 128
TOP = 8
SLOTS = 8
bf16 = jnp.bfloat16
f32 = jnp.float32


def params(mib):
    return pltpu.CompilerParams(vmem_limit_bytes=mib * 1024 * 1024)


def iota(shape, dim):
    return lax.broadcasted_iota(jnp.int32, shape, dim)


def ones(where):
    return jnp.where(where, jnp.float32(1.0), jnp.float32(0.0)).astype(bf16)


def dot(a, b, dims=((1,), (0,))):
    return lax.dot_general(a, b, (dims, ((), ())), preferred_element_type=f32)


def prepare_kernel(
    q_ref, k_ref, v_ref, res_ref, flag_ref, ids_ref, gates_ref, out_ref, own_ref, pick_ref, table_ref
):
    rows, cols = q_ref.shape
    experts, most = table_ref.shape

    @pl.when(pl.program_id(0) == 0)
    def _():
        flags = ones(jnp.broadcast_to(flag_ref[...], (rows, rows)) == 1)
        upper = ones(iota((rows, rows), 0) < iota((rows, rows), 1))
        lower = ones(iota((rows, rows), 0) > iota((rows, rows), 1))
        eye = ones(iota((rows, rows), 0) == iota((rows, rows), 1))
        rank = dot(flags, upper)[:1].astype(jnp.int32)
        pick = ones((iota((most, rows), 0) == rank) & (flag_ref[...] == 1))
        pick_ref[...] = pick
        masked = dot(eye, flags, ((1,), (1,)))[:, :1] > 0.5
        named = jnp.zeros((rows, experts), f32)
        gates = jnp.zeros((rows, experts), f32)
        for k in range(TOP):
            hit = (ids_ref[:, k : k + 1] == iota((rows, experts), 1)) & masked
            named = jnp.where(hit, 1.0, named)
            gates = jnp.where(hit, gates_ref[:, k : k + 1], gates)
        place = (named * (dot(lower, named.astype(bf16)) + 1.0)).astype(bf16)
        high = gates.astype(bf16)
        own_ref[0] = place
        own_ref[1] = high
        own_ref[2] = (gates - high.astype(f32)).astype(bf16)
        table_ref[...] = dot(place, pick, ((0,), (1,))).astype(bf16)

    out_ref[0, :rows] = q_ref[...]
    out_ref[0, rows : 2 * rows] = k_ref[...]
    out_ref[0, 2 * rows : 3 * rows] = v_ref[...]
    out_ref[0, 3 * rows : 3 * rows + most] = dot(pick_ref[...], res_ref[...]).astype(bf16)
    extra = 3 * rows + most
    numbers = iota((16, rows), 1).astype(f32).astype(bf16)
    spot = dot(numbers, pick_ref[...], ((1,), (1,))).astype(bf16)
    count = dot(jnp.ones((16, rows), bf16), pick_ref[...], ((1,), (1,)))
    spot = jnp.where(count > 0.5, spot.astype(f32), -1.0).astype(bf16)
    out_ref[0, extra:] = jnp.zeros((16, cols), bf16)
    for h in range(experts // 16):
        out_ref[0, extra:, h * 128 : h * 128 + most] = table_ref[h * 16 : (h + 1) * 16]
        out_ref[0, extra:, h * 128 + 64 : h * 128 + 64 + most] = spot


def prepare(q, k, v, res, flags, ids, gates, groups, experts, most):
    rows, width = q.shape
    cols = width // groups
    total = 3 * rows + most + 16
    piece = pl.BlockSpec((rows, cols), lambda j: (0, j))
    return pl.pallas_call(
        prepare_kernel,
        grid=(groups,),
        in_specs=[
            piece,
            piece,
            piece,
            piece,
            pl.BlockSpec((1, rows), lambda j: (0, 0)),
            pl.BlockSpec((rows, TOP), lambda j: (0, 0)),
            pl.BlockSpec((rows, TOP), lambda j: (0, 0)),
        ],
        out_specs=[
            pl.BlockSpec((1, total, cols), lambda j: (j, 0, 0)),
            pl.BlockSpec((3, rows, experts), lambda j: (0, 0, 0)),
        ],
        out_shape=[
            jax.ShapeDtypeStruct((groups, total, cols), bf16),
            jax.ShapeDtypeStruct((3, rows, experts), bf16),
        ],
        scratch_shapes=[pltpu.VMEM((most, rows), bf16), pltpu.VMEM((experts, most), bf16)],
        compiler_params=params(60),
        name="prepare",
    )(q, k, v, res, flags, ids, gates)


def attend_kernel(
    in_ref, table_ref, gain_ref, attn_ref, first_ref, second_ref, place_ref, spot_ref, v_ref
):
    blocks, rows, cols = attn_ref.shape
    experts = first_ref.shape[0]
    most = spot_ref.shape[2]
    length = blocks * rows
    heads = cols // HEAD_DIM
    part = SLOTS // 2

    @pl.when(pl.program_id(0) == 0)
    def _():
        inner = iota((16, SLOTS, 2 * most), 1)
        mine = inner // part == iota((16, SLOTS, 2 * most), 2) // most
        slot = (inner % part + 1).astype(f32)
        for b in range(0, blocks, 2):
            for h in range(experts // 16):
                here = slice(h * 128, h * 128 + most)
                pair = [table_ref[b + i, :, here].astype(f32) for i in range(2)]
                table = jnp.concatenate(pair, axis=1)[:, None, :]
                for q in range(2):
                    hit = jnp.where(mine & (table == slot + q * part), 1.0, 0.0)
                    hit = hit.reshape(128, 2 * most).astype(bf16)
                    place_ref[q, b // 2, h * 128 : (h + 1) * 128] = hit
            for i in range(2):
                spot = table_ref[b + i, :, 64 : 64 + most].astype(f32)[:1]
                spot_ref[b + i] = ones(iota((rows, most), 0).astype(f32) == spot)
        v_ref[:, HEAD_DIM:] = jnp.ones((length, HEAD_DIM), bf16)

    scale = math.log2(math.e) / math.sqrt(HEAD_DIM)
    gain = gain_ref[...].astype(f32)
    step = 2
    for h in range(heads):
        here = slice(h * HEAD_DIM, (h + 1) * HEAD_DIM)
        k_all = in_ref[:, rows : 2 * rows, here].reshape(length, HEAD_DIM)
        v_ref[:, :HEAD_DIM] = in_ref[:, 2 * rows : 3 * rows, here].reshape(length, HEAD_DIM)
        for first in range(0, blocks, step):
            q_part = in_ref[first : first + step, :rows, here].reshape(step * rows, HEAD_DIM)
            scores = dot(q_part, k_all, ((1,), (1,)))
            peak = jnp.max(scores, axis=-1, keepdims=True)
            expo = jnp.exp2((scores - peak) * scale).astype(bf16)
            mixed = dot(expo, v_ref[...])
            attn = (mixed[:, :HEAD_DIM] / mixed[:, HEAD_DIM:]).astype(bf16)
            attn_ref[first : first + step, :, here] = attn.reshape(step, rows, HEAD_DIM)
    for b in range(0, blocks, 2):
        pair = []
        for i in range(b, b + 2):
            hidden = dot(spot_ref[i], attn_ref[i], ((0,), (0,)))
            hidden += in_ref[i, 3 * rows : 3 * rows + most].astype(f32)
            pair.append((hidden * gain).astype(bf16))
        both = jnp.concatenate(pair, axis=0)
        for q, out_ref in enumerate((first_ref, second_ref)):
            sent = dot(place_ref[q, b // 2], both)
            sent = sent.reshape(experts, SLOTS, cols).astype(bf16)
            out_ref[:, 0, b // 2] = sent
            out_ref[:, 1, b // 2] = sent


def attend(pieces, gain, rows, experts, heads=2):
    blocks, total, cols = pieces.shape
    most = total - 3 * rows - 16
    span = heads * HEAD_DIM
    sent = pl.BlockSpec((experts, 2, blocks // 2, SLOTS, span), lambda h: (0, 0, 0, 0, h))
    return pl.pallas_call(
        attend_kernel,
        grid=(cols // span,),
        in_specs=[
            pl.BlockSpec((blocks, total, span), lambda h: (0, 0, h)),
            pl.BlockSpec((blocks, 16, cols), lambda h: (0, total // 16 - 1, 0)),
            pl.BlockSpec((1, span), lambda h: (0, h)),
        ],
        out_specs=[pl.BlockSpec((blocks, rows, span), lambda h: (0, 0, h)), sent, sent],
        out_shape=[
            jax.ShapeDtypeStruct((blocks, rows, cols), bf16),
            jax.ShapeDtypeStruct((experts, 2, blocks // 2, SLOTS, cols), bf16),
            jax.ShapeDtypeStruct((experts, 2, blocks // 2, SLOTS, cols), bf16),
        ],
        scratch_shapes=[
            pltpu.VMEM((2, blocks // 2, experts * SLOTS, 2 * most), bf16),
            pltpu.VMEM((blocks, rows, most), bf16),
            pltpu.VMEM((blocks * rows, 2 * HEAD_DIM), bf16),
        ],
        compiler_params=params(60),
        name="attend",
    )(pieces, pieces, gain)


def open_kernel(rows_ref, gain_ref, gate_ref, up_ref, out_ref, scale_ref):
    groups, count, per, cols = rows_ref.shape
    total = count * per

    @pl.when(pl.program_id(0) == 0)
    def _():
        back = 1.0 / gain_ref[...].astype(f32)
        square = jnp.zeros((total, 128), f32)
        for g in range(groups):
            hidden = rows_ref[g].reshape(total, cols).astype(f32)
            hidden = hidden * back[:, g * cols : (g + 1) * cols]
            for c in range(0, cols, 128):
                square += hidden[:, c : c + 128] * hidden[:, c : c + 128]
        mean = jnp.sum(square, axis=-1, keepdims=True) / (groups * cols)
        scale_ref[...] = lax.rsqrt(mean + 1e-06)

    gate_part = jnp.zeros((total, out_ref.shape[1]), f32)
    up_part = jnp.zeros((total, out_ref.shape[1]), f32)
    for g in range(groups):
        x = rows_ref[g].reshape(total, cols)
        gate_part += dot(x, gate_ref[g * cols : (g + 1) * cols])
        up_part += dot(x, up_ref[g * cols : (g + 1) * cols])
    gate_part = gate_part * scale_ref[...]
    act = gate_part / (1.0 + jnp.exp(-gate_part)) * (up_part * scale_ref[...])
    out_ref[...] = act.astype(bf16)


def expert_open(arrived, gain, gate, up):
    groups, count, per, cols = arrived.shape
    width, half = gate.shape
    total = count * per
    span = 256
    weight = pl.BlockSpec((width, span), lambda n: (0, n))
    return pl.pallas_call(
        open_kernel,
        grid=(half // span,),
        in_specs=[
            pl.BlockSpec((groups, count, per, cols), lambda n: (0, 0, 0, 0)),
            pl.BlockSpec((1, width), lambda n: (0, 0)),
            weight,
            weight,
        ],
        out_specs=pl.BlockSpec((total, span), lambda n: (0, n)),
        out_shape=jax.ShapeDtypeStruct((total, half), bf16),
        scratch_shapes=[pltpu.VMEM((total, 1), f32)],
        compiler_params=params(60),
        cost_estimate=pl.CostEstimate(
            flops=4 * total * width * half,
            bytes_accessed=4 * width * half + 2 * total * (width + half),
            transcendentals=total * half,
        ),
        name="expert_open",
    )(arrived, gain, gate, up)


def close_kernel(
    side_ref, mine_ref, other_ref, own_a, own_b, far_a, far_b, out_ref
):
    del side_ref
    groups, count, _, span = out_ref.shape
    left = dot(mine_ref[...], own_a[...]) + dot(other_ref[...], far_a[...])
    right = dot(mine_ref[...], own_b[...]) + dot(other_ref[...], far_b[...])
    total = left.shape[0]
    part = SLOTS // 2
    low = iota((total, span), 0) % SLOTS < part
    even = jnp.where(low, left, pltpu.roll(right, part, 0))
    odd = jnp.where(low, pltpu.roll(left, total - part, 0), right)
    for i, tile in enumerate((even, odd)):
        tile = tile.reshape(count, groups // 2, SLOTS, span).astype(bf16)
        for p in range(count):
            for b in range(groups // 2):
                out_ref[2 * b + i, p] = tile[p, b]


def expert_close(side, mine, other, down, far, groups, count):
    total, half = mine.shape
    width = far.shape[1]
    span = 512
    steps = width // 2 // span
    act = pl.BlockSpec((total, half), lambda c, side: (0, 0))

    def own(shift):
        return pl.BlockSpec((half, span), lambda c, side: (0, side[0] * 2 * steps + shift + c))

    def recv(shift):
        return pl.BlockSpec((half, span), lambda c, side: (0, shift + c))

    return pl.pallas_call(
        close_kernel,
        grid_spec=pltpu.PrefetchScalarGridSpec(
            num_scalar_prefetch=1,
            grid=(steps,),
            in_specs=[act, act, own(0), own(steps), recv(0), recv(steps)],
            out_specs=pl.BlockSpec((groups, count, SLOTS, span), lambda c, side: (0, 0, 0, c)),
        ),
        out_shape=jax.ShapeDtypeStruct((groups, count, SLOTS, width // 2), bf16),
        compiler_params=params(60),
        cost_estimate=pl.CostEstimate(
            flops=4 * total * width * half,
            bytes_accessed=2 * (2 * width * half + total * (2 * half + width)),
            transcendentals=0,
        ),
        name="expert_close",
    )(side, mine, other, down, down, far, far)


def combine_kernel(first_ref, second_ref, own_ref, attn_ref, res_ref, cached_ref, out_ref, mix_ref):
    rows, experts = own_ref.shape[1:]
    per = first_ref.shape[2]
    slots = experts * per
    part = SLOTS // 2
    step = pl.program_id(0)

    @pl.when(step == 0)
    def _():
        spread = ones(iota((experts, slots), 0) == iota((experts, slots), 1) // per)
        place = dot(own_ref[0], spread)
        high = dot(own_ref[1], spread)
        low = dot(own_ref[2], spread)
        inner = iota((rows, slots), 1) % per
        for side in range(2):
            for q in range(2):
                slot = (inner % part + 1 + q * part).astype(f32)
                hit = (inner // part == side) & (place == slot)
                mix_ref[side, q, :rows] = jnp.where(hit, high, 0.0).astype(bf16)
                mix_ref[side, q, rows:] = jnp.where(hit, low, 0.0).astype(bf16)

    side = step % 2
    cols = out_ref.shape[1]
    both = dot(mix_ref[side, 0], first_ref[:, 0].reshape(slots, cols))
    both += dot(mix_ref[side, 1], second_ref[:, 0].reshape(slots, cols))
    mixed = both[:rows] + both[rows:]
    masked = jnp.max(own_ref[0].astype(f32), axis=-1, keepdims=True) > 0.5
    moe = jnp.where(masked, mixed, cached_ref[...].astype(f32))
    merge, _, piece = attn_ref.shape
    for m in range(merge):
        here = slice(m * piece, (m + 1) * piece)
        hid = res_ref[:, here].astype(f32) + attn_ref[m].astype(f32)
        out_ref[:, here] = (hid + moe[:, here]).astype(bf16)


def combine(first, second, own, attn, residual, cached):
    experts, _, per, cols = first.shape
    groups, rows, piece = attn.shape
    width = groups * piece
    merge = cols // piece
    flat = pl.BlockSpec((rows, cols), lambda j: (0, j))
    back = pl.BlockSpec((experts, 1, per, cols), lambda j: (0, j // 2, 0, 0))
    return pl.pallas_call(
        combine_kernel,
        grid=(width // cols,),
        in_specs=[
            back,
            back,
            pl.BlockSpec(own.shape, lambda j: (0, 0, 0)),
            pl.BlockSpec((merge, rows, piece), lambda j: (j, 0, 0)),
            flat,
            flat,
        ],
        out_specs=flat,
        out_shape=jax.ShapeDtypeStruct((rows, width), bf16),
        scratch_shapes=[pltpu.VMEM((2, 2, 2 * rows, experts * per), bf16)],
        compiler_params=params(60),
        name="combine",
    )(first, second, own, attn, residual, cached)


def exchange(blocks, axes):
    return lax.all_to_all(blocks, axes, split_axis=0, concat_axis=0, tiled=True)


def home(blocks):
    count = blocks.shape[0]
    here = lax.axis_index("seq")
    parts = [lax.dynamic_index_in_dim(blocks, here, 0, keepdims=False)]
    for d in range(1, count):
        part = lax.dynamic_index_in_dim(blocks, (here + d) % count, 0, keepdims=False)
        parts.append(lax.ppermute(part, "seq", [(i, (i + d) % count) for i in range(count)]))
    order = (here - jnp.arange(count, dtype=jnp.int32)) % count
    return jnp.stack(parts)[order]


def per_device(
    queries,
    keys,
    values,
    residual_in,
    cached_moe,
    norm_gain,
    still_masked,
    expert_ids,
    gate_weights,
    w_gate,
    w_up,
    w_down,
):
    rows, width = queries.shape[1:]
    seq_count = lax.axis_size("seq")
    exp_count = lax.axis_size("exp")
    devices = seq_count * exp_count
    experts = devices // 2
    cols = width // seq_count
    most = rows * 3 // 8

    pieces, own = prepare(
        queries[0],
        keys[0],
        values[0],
        residual_in[0],
        still_masked,
        expert_ids[0],
        gate_weights[0],
        seq_count,
        experts,
        most,
    )
    pieces = exchange(pieces, "seq")
    gain = norm_gain[None, :]
    own_gain = lax.dynamic_slice_in_dim(gain, lax.axis_index("seq") * cols, cols, 1)

    exp_index = lax.axis_index("exp")
    side = exp_index % 2
    partner = [(p, p ^ 1) for p in range(exp_count)]
    far = lax.dynamic_slice_in_dim(w_down[0], (1 - side) * (width // 2), width // 2, 1)
    far = lax.ppermute(far, "exp", partner)

    attn, *sent = attend(pieces, own_gain, rows, experts)
    per = seq_count * SLOTS // 2
    sent = [part.reshape(devices, per, cols) for part in sent]
    first = exchange(sent[0], ("seq", "exp"))
    first, sent[1] = lax.optimization_barrier((first, sent[1]))
    second = exchange(sent[1], ("seq", "exp"))

    def experts_on(arrived):
        arrived = arrived.reshape(seq_count, exp_count, per, cols)
        mine = expert_open(arrived, gain, w_gate[0], w_up[0])
        other = lax.ppermute(mine, "exp", partner)
        done = expert_close(side[None], mine, other, w_down[0], far, seq_count, exp_count)
        return done.reshape(devices, SLOTS, width // 4)

    attn = home(attn)
    back = []
    for arrived in (first, second):
        done = experts_on(arrived)
        back.append(exchange(done, ("seq", "exp")).reshape(experts, 2, SLOTS, width // 4))
    out = combine(*back, own, attn, residual_in[0], cached_moe[0])
    return out[None]


def solution(mesh):
    return jax.shard_map(
        per_device,
        mesh=mesh,
        in_specs=(
            P("exp", "seq", None),
            P("exp", "seq", None),
            P("exp", "seq", None),
            P("exp", "seq", None),
            P("exp", "seq", None),
            P(),
            P("exp", "seq"),
            P("exp", "seq", None),
            P("exp", "seq", None),
            P(("seq", "exp"), None, None),
            P(("seq", "exp"), None, None),
            P(("seq", "exp"), None, None),
        ),
        out_specs=P("exp", "seq", None),
        check_vma=False,
    )
```

```python
import math

import jax
import jax.numpy as jnp
from jax import lax
from jax.experimental import pallas as pl
from jax.experimental.pallas import tpu as pltpu
from jax.sharding import PartitionSpec as P

HEAD_DIM = 128
TOP = 8
SLOTS = 8
bf16 = jnp.bfloat16
f32 = jnp.float32


def params(mib):
    return pltpu.CompilerParams(vmem_limit_bytes=mib * 1024 * 1024)


def iota(shape, dim):
    return lax.broadcasted_iota(jnp.int32, shape, dim)


def ones(where):
    return jnp.where(where, jnp.float32(1.0), jnp.float32(0.0)).astype(bf16)


def dot(a, b, dims=((1,), (0,))):
    return lax.dot_general(a, b, (dims, ((), ())), preferred_element_type=f32)


def split_kernel(side_ref, down_ref, *far_refs):
    del side_ref
    step = pl.program_id(0)
    for i, far_ref in enumerate(far_refs):

        @pl.when(step == i)
        def _(far_ref=far_ref):
            far_ref[...] = down_ref[...]


def split(side, down, parts):
    half, width = down.shape
    span = width // 2 // parts
    return pl.pallas_call(
        split_kernel,
        grid_spec=pltpu.PrefetchScalarGridSpec(
            num_scalar_prefetch=1,
            grid=(parts,),
            in_specs=[pl.BlockSpec((half, span), lambda c, side: (0, (1 - side[0]) * parts + c))],
            out_specs=[pl.BlockSpec((half, span), lambda c, side: (0, 0))] * parts,
        ),
        out_shape=[jax.ShapeDtypeStruct((half, span), bf16)] * parts,
        compiler_params=params(60),
        name="split",
    )(side, down)


def prepare_kernel(
    q_ref,
    k_ref,
    v_ref,
    res_ref,
    flag_ref,
    ids_ref,
    gates_ref,
    out_ref,
    own_ref,
    pick_ref,
    table_ref,
):
    rows = q_ref.shape[0]
    merge, _, cols = out_ref.shape
    experts, most = table_ref.shape
    extra = 3 * rows + most

    @pl.when(pl.program_id(0) == 0)
    def _():
        upper = ones(iota((rows, rows), 0) < iota((rows, rows), 1))
        masked = flag_ref[...] == 1
        rank = dot(ones(jnp.broadcast_to(flag_ref[...], (16, rows)) == 1), upper)[:1]
        pick = ones((iota((most, rows), 0).astype(f32) == rank) & masked)
        pick_ref[...] = pick
        named = jnp.zeros((experts, rows), f32)
        gates = jnp.zeros((experts, rows), f32)
        for k in range(TOP):
            hit = (ids_ref[k : k + 1, :] == iota((experts, rows), 0)) & masked
            named = jnp.where(hit, 1.0, named)
            gates = jnp.where(hit, gates_ref[k : k + 1, :], gates)
        place = (named * (dot(named.astype(bf16), upper) + 1.0)).astype(bf16)
        high = gates.astype(bf16)
        own_ref[0] = place
        own_ref[1] = high
        own_ref[2] = (gates - high.astype(f32)).astype(bf16)
        table_ref[...] = dot(place, pick, ((1,), (1,))).astype(bf16)

    numbers = iota((16, rows), 1).astype(f32).astype(bf16)
    spot = dot(numbers, pick_ref[...], ((1,), (1,)))
    count = dot(jnp.ones((16, rows), bf16), pick_ref[...], ((1,), (1,)))
    spot = jnp.where(count > 0.5, spot, -1.0).astype(bf16)
    for m in range(merge):
        here = slice(m * cols, (m + 1) * cols)
        out_ref[m, :rows] = q_ref[:, here]
        out_ref[m, rows : 2 * rows] = k_ref[:, here]
        out_ref[m, 2 * rows : 3 * rows] = v_ref[:, here]
        out_ref[m, 3 * rows : extra] = dot(pick_ref[...], res_ref[:, here]).astype(bf16)
        out_ref[m, extra:] = jnp.zeros((16, cols), bf16)
        for h in range(experts // 16):
            out_ref[m, extra:, h * 128 : h * 128 + most] = table_ref[h * 16 : (h + 1) * 16]
            out_ref[m, extra:, h * 128 + 64 : h * 128 + 64 + most] = spot


def prepare(q, k, v, res, flags, ids, gates, groups, experts, most):
    rows, width = q.shape
    cols = width // groups
    total = 3 * rows + most + 16
    merge = 2
    piece = pl.BlockSpec((rows, merge * cols), lambda j: (0, j))
    return pl.pallas_call(
        prepare_kernel,
        grid=(groups // merge,),
        in_specs=[
            piece,
            piece,
            piece,
            piece,
            pl.BlockSpec((1, rows), lambda j: (0, 0)),
            pl.BlockSpec((TOP, rows), lambda j: (0, 0)),
            pl.BlockSpec((TOP, rows), lambda j: (0, 0)),
        ],
        out_specs=[
            pl.BlockSpec((merge, total, cols), lambda j: (j, 0, 0)),
            pl.BlockSpec((3, experts, rows), lambda j: (0, 0, 0)),
        ],
        out_shape=[
            jax.ShapeDtypeStruct((groups, total, cols), bf16),
            jax.ShapeDtypeStruct((3, experts, rows), bf16),
        ],
        scratch_shapes=[pltpu.VMEM((most, rows), bf16), pltpu.VMEM((experts, most), bf16)],
        compiler_params=params(60),
        name="prepare",
    )(q, k, v, res, flags, ids, gates)


def attend_kernel(in_ref, table_ref, gain_ref, attn_ref, out_ref, place_ref, spot_ref, v_ref):
    cores, chips, rows, cols = attn_ref.shape
    blocks = cores * chips
    experts = out_ref.shape[0]
    most = spot_ref.shape[2]
    length = blocks * rows
    heads = cols // HEAD_DIM

    @pl.when(pl.program_id(0) == 0)
    def _():
        wanted = iota((16, SLOTS, most), 1).astype(f32) + 1.0
        for b in range(blocks):
            for h in range(experts // 16):
                table = table_ref[b, :, h * 128 : h * 128 + most].astype(f32)
                hit = jnp.where(table[:, None, :] == wanted, 1.0, 0.0)
                place_ref[b, h * 128 : (h + 1) * 128] = hit.reshape(128, most).astype(bf16)
            spot = table_ref[b, :, 64 : 64 + most].astype(f32)[:1]
            spot_ref[b] = ones(iota((rows, most), 0).astype(f32) == spot)
        v_ref[:, HEAD_DIM:] = jnp.ones((length, HEAD_DIM), bf16)

    scale = math.log2(math.e) / math.sqrt(HEAD_DIM)
    gain = gain_ref[...].astype(f32)
    step = 2
    for h in range(heads):
        here = slice(h * HEAD_DIM, (h + 1) * HEAD_DIM)
        k_all = in_ref[:, rows : 2 * rows, here].reshape(length, HEAD_DIM)
        v_ref[:, :HEAD_DIM] = in_ref[:, 2 * rows : 3 * rows, here].reshape(length, HEAD_DIM)
        for first in range(0, blocks, step):
            q_part = in_ref[first : first + step, :rows, here].reshape(step * rows, HEAD_DIM)
            scores = dot(q_part, k_all, ((1,), (1,)))
            peak = jnp.max(scores, axis=-1, keepdims=True)
            expo = jnp.exp2((scores - peak) * scale).astype(bf16)
            mixed = dot(expo, v_ref[...])
            attn = (mixed[:, :HEAD_DIM] / mixed[:, HEAD_DIM:]).astype(bf16)
            attn_ref[:, first // 2, :, here] = attn.reshape(step, rows, HEAD_DIM)
    for b in range(blocks):
        hidden = dot(spot_ref[b], attn_ref[b % 2, b // 2], ((0,), (0,)))
        hidden += in_ref[b, 3 * rows : 3 * rows + most].astype(f32)
        sent = dot(place_ref[b], (hidden * gain).astype(bf16))
        sent = sent.reshape(experts, SLOTS, cols).astype(bf16)
        out_ref[:, 0, b] = sent
        out_ref[:, 1, b] = sent


def attend(pieces, gain, rows, experts, heads=2):
    blocks, total, cols = pieces.shape
    most = total - 3 * rows - 16
    span = heads * HEAD_DIM
    return pl.pallas_call(
        attend_kernel,
        grid=(cols // span,),
        in_specs=[
            pl.BlockSpec((blocks, total, span), lambda h: (0, 0, h)),
            pl.BlockSpec((blocks, 16, cols), lambda h: (0, total // 16 - 1, 0)),
            pl.BlockSpec((1, span), lambda h: (0, h)),
        ],
        out_specs=[
            pl.BlockSpec((2, blocks // 2, rows, span), lambda h: (0, 0, 0, h)),
            pl.BlockSpec((experts, 2, blocks, SLOTS, span), lambda h: (0, 0, 0, 0, h)),
        ],
        out_shape=[
            jax.ShapeDtypeStruct((2, blocks // 2, rows, cols), bf16),
            jax.ShapeDtypeStruct((experts, 2, blocks, SLOTS, cols), bf16),
        ],
        scratch_shapes=[
            pltpu.VMEM((blocks, experts * SLOTS, most), bf16),
            pltpu.VMEM((blocks, rows, most), bf16),
            pltpu.VMEM((blocks * rows, 2 * HEAD_DIM), bf16),
        ],
        compiler_params=params(60),
        name="attend",
    )(pieces, pieces, gain)


def open_kernel(rows_ref, gain_ref, gate_ref, up_ref, *rest):
    *out_refs, gates_ref, ups_ref, square_ref = rest
    step = pl.program_id(0)
    merge, count, per, cols = rows_ref.shape
    total = count * per
    half = gate_ref.shape[1]
    back = 1.0 / gain_ref[...].astype(f32)
    square = jnp.zeros((total, 128), f32)
    gate_part = jnp.zeros((total, half), f32)
    up_part = jnp.zeros((total, half), f32)
    for m in range(merge):
        here = slice(m * cols, (m + 1) * cols)
        x = rows_ref[m].reshape(total, cols)
        gate_part += dot(x, gate_ref[here])
        up_part += dot(x, up_ref[here])
        hidden = x.astype(f32) * back[:, here]
        for c in range(0, cols, 128):
            square += hidden[:, c : c + 128] * hidden[:, c : c + 128]

    @pl.when(step == 0)
    def _():
        square_ref[...] = square
        gates_ref[...] = gate_part
        ups_ref[...] = up_part

    @pl.when(step > 0)
    def _():
        square_ref[...] += square
        gates_ref[...] += gate_part
        ups_ref[...] += up_part

    @pl.when(step == pl.num_programs(0) - 1)
    def _():
        width = pl.num_programs(0) * merge * cols
        mean = jnp.sum(square_ref[...], axis=-1, keepdims=True) / width
        scale = lax.rsqrt(mean + 1e-06)
        gate_full = gates_ref[...] * scale
        act = gate_full / (1.0 + jnp.exp(-gate_full)) * (ups_ref[...] * scale)
        act = act.astype(bf16).reshape(count, per, half)
        piece = per // len(out_refs)
        for i, out_ref in enumerate(out_refs):
            out_ref[...] = act[:, i * piece : (i + 1) * piece].reshape(count * piece, half)


def expert_open(arrived, part, pieces, gain, gate, up):
    groups, count, _, cols = arrived.shape
    per = 2 * SLOTS * pieces
    width, half = gate.shape
    total = count * per
    merge = 2
    weight = pl.BlockSpec((merge * cols, half), lambda n: (n, 0))
    return pl.pallas_call(
        open_kernel,
        grid=(groups // merge,),
        in_specs=[
            pl.BlockSpec((merge, count, per, cols), lambda n: (n, 0, part, 0)),
            pl.BlockSpec((1, merge * cols), lambda n: (0, n)),
            weight,
            weight,
        ],
        out_specs=[pl.BlockSpec((total // pieces, half), lambda n: (0, 0))] * pieces,
        out_shape=[jax.ShapeDtypeStruct((total // pieces, half), bf16)] * pieces,
        scratch_shapes=[
            pltpu.VMEM((total, half), f32),
            pltpu.VMEM((total, half), f32),
            pltpu.VMEM((total, 128), f32),
        ],
        compiler_params=params(20),
        cost_estimate=pl.CostEstimate(
            flops=4 * total * width * half,
            bytes_accessed=4 * width * half + 2 * total * (width + half),
            transcendentals=total * half,
        ),
        name="expert_open",
    )(arrived, gain, gate, up)


def close_kernel(side_ref, mine_ref, other_ref, own_ref, *rest):
    del side_ref
    out_ref = rest[-1]
    step = pl.program_id(0)
    merge, count, _, span = out_ref.shape
    parts = 2
    for i in range(parts):

        @pl.when(step // 2 == i)
        def _(far_ref=rest[i]):
            result = dot(mine_ref[...], own_ref[...]) + dot(other_ref[...], far_ref[...])
            result = result.reshape(count, merge, SLOTS, span).astype(bf16)
            for m in range(merge):
                out_ref[m] = result[:, m]


def expert_close(side, mine, other, down, far, part, groups, count, done):
    total, half = mine.shape
    width = down.shape[1] // 2
    steps = 2 * len(far)
    span = width // steps
    merge = total // (count * SLOTS)
    act = pl.BlockSpec((total, half), lambda c, side: (0, 0))
    held = [] if done is None else [done]
    return pl.pallas_call(
        close_kernel,
        grid_spec=pltpu.PrefetchScalarGridSpec(
            num_scalar_prefetch=1,
            grid=(steps,),
            in_specs=[
                act,
                act,
                pl.BlockSpec((half, span), lambda c, side: (0, side[0] * steps + c)),
            ]
            + [
                pl.BlockSpec((half, span), lambda c, side, i=i: (0, jnp.clip(c - 2 * i, 0, 1)))
                for i in range(len(far))
            ]
            + [pl.BlockSpec(memory_space=pl.ANY)] * len(held),
            out_specs=pl.BlockSpec((merge, count, SLOTS, span), lambda c, side: (part, 0, 0, c)),
        ),
        out_shape=jax.ShapeDtypeStruct((groups, count, SLOTS, width), bf16),
        input_output_aliases={4 + len(far): 0} if held else {},
        compiler_params=params(20),
        cost_estimate=pl.CostEstimate(
            flops=4 * total * width * half,
            bytes_accessed=2 * (2 * width * half + total * (2 * half + width)),
            transcendentals=0,
        ),
        name="expert_close",
    )(side, mine, other, down, *far, *held)


def combine_kernel(chip_ref, back_ref, own_ref, res_ref, cached_ref, *rest):
    del chip_ref
    *attn_refs, out_ref, mix_ref = rest
    step = pl.program_id(0)
    _, experts, rows = own_ref.shape
    slots = experts * SLOTS
    cols = out_ref.shape[1]

    @pl.when(step == 0)
    def _():
        spread = ones(iota((experts, slots), 0) == iota((experts, slots), 1) // SLOTS)
        slot = (iota((rows, slots), 1) % SLOTS + 1).astype(f32)
        hit = dot(own_ref[0], spread, ((0,), (0,))) == slot
        for i in range(2):
            gates = dot(own_ref[1 + i], spread, ((0,), (0,)))
            mix_ref[i * rows : (i + 1) * rows] = jnp.where(hit, gates, 0.0).astype(bf16)

    both = dot(mix_ref[...], back_ref[:, 0].reshape(slots, cols))
    mixed = both[:rows] + both[rows:]
    named = dot(own_ref[0], jnp.ones((experts, 128), bf16), ((0,), (0,)))
    moe = jnp.where(named[:, :1] > 0.5, mixed, cached_ref[...].astype(f32))
    for i, attn_ref in enumerate(attn_refs):

        @pl.when(step == i)
        def _(attn_ref=attn_ref):
            merge, _, piece = attn_ref.shape
            for m in range(merge):
                here = slice(m * piece, (m + 1) * piece)
                hid = res_ref[:, here].astype(f32) + attn_ref[m].astype(f32)
                out_ref[:, here] = (hid + moe[:, here]).astype(bf16)


def combine(chip, back, own, attn, residual, cached):
    experts, sides, _, half = back.shape
    merge, rows, piece = attn[0].shape
    chips = len(attn)
    span = merge * piece
    steps = half // span

    def place(i, chip):
        return lax.rem(chip[0] + chips - i, chips)

    flat = pl.BlockSpec((rows, span), lambda i, chip: (0, place(i, chip)))
    back_spec = pl.BlockSpec(
        (experts, 1, SLOTS, span),
        lambda i, chip: (0, lax.div(place(i, chip), steps), 0, lax.rem(place(i, chip), steps)),
    )
    return pl.pallas_call(
        combine_kernel,
        grid_spec=pltpu.PrefetchScalarGridSpec(
            num_scalar_prefetch=1,
            grid=(chips,),
            in_specs=[back_spec, pl.BlockSpec(own.shape, lambda i, chip: (0, 0, 0)), flat, flat]
            + [pl.BlockSpec((merge, rows, piece), lambda i, chip: (0, 0, 0))] * chips,
            out_specs=flat,
            scratch_shapes=[pltpu.VMEM((2 * rows, experts * SLOTS), bf16)],
        ),
        out_shape=jax.ShapeDtypeStruct((rows, chips * span), bf16),
        compiler_params=params(60),
        name="combine",
    )(chip, back, own, residual, cached, *attn)


def home(attn):
    chips = attn.shape[1]
    count = 2 * chips
    here = lax.axis_index("seq")
    core = here % 2
    keep = lax.dynamic_index_in_dim(attn, core, 0, keepdims=False)
    give = lax.dynamic_index_in_dim(attn, 1 - core, 0, keepdims=False)
    took = lax.ppermute(give, "seq", [(i, i ^ 1) for i in range(count)])
    lower = jnp.where(core == 0, keep, took)
    upper = jnp.where(core == 0, took, keep)
    both = jnp.stack([lower, upper], axis=1)
    chip = here // 2
    parts = []
    for d in range(chips):
        part = lax.dynamic_index_in_dim(both, (chip + d) % chips, 0, keepdims=False)
        if d:
            hops = [(i, (i + 2 * d) % count) for i in range(count)]
            part = lax.ppermute(part, "seq", hops)
        parts.append(part)
    return parts


def exchange(blocks, axes):
    return lax.all_to_all(blocks, axes, split_axis=0, concat_axis=0, tiled=True)


def per_device(
    queries,
    keys,
    values,
    residual_in,
    cached_moe,
    norm_gain,
    still_masked,
    expert_ids,
    gate_weights,
    w_gate,
    w_up,
    w_down,
):
    rows, width = queries.shape[1:]
    seq_count = lax.axis_size("seq")
    exp_count = lax.axis_size("exp")
    devices = seq_count * exp_count
    experts = devices // 2
    cols = width // seq_count
    most = rows * 3 // 8
    all_axes = ("seq", "exp")
    partner = [(p, p ^ 1) for p in range(exp_count)]
    side = (lax.axis_index("exp") % 2)[None].astype(jnp.int32)
    gain = norm_gain[None, :]
    own_gain = lax.dynamic_slice_in_dim(gain, lax.axis_index("seq") * cols, cols, 1)

    far = split(side, w_down[0], 2)
    *far, queries = lax.optimization_barrier((*far, queries))
    far = [lax.ppermute(part, "exp", partner) for part in far]
    pieces, own = prepare(
        queries[0],
        keys[0],
        values[0],
        residual_in[0],
        still_masked,
        expert_ids[0].T,
        gate_weights[0].T,
        seq_count,
        experts,
        most,
    )
    pieces = exchange(pieces, "seq")
    tied = lax.optimization_barrier((pieces, gain, own_gain, far[0]))
    pieces, gain, own_gain, far[0] = tied

    attn, sent = attend(pieces, own_gain, rows, experts)
    sent, far[1] = lax.optimization_barrier((sent, far[1]))
    arrived = exchange(sent.reshape(devices, seq_count * SLOTS, cols), all_axes)
    arrived = arrived.reshape(seq_count, exp_count, seq_count * SLOTS, cols)

    def opened(part):
        return expert_open(arrived, part, 1, gain, w_gate[0], w_up[0])[0]

    def closed(part, mine, done):
        other = lax.ppermute(mine, "exp", partner)
        return expert_close(side, mine, other, w_down[0], far, part, seq_count, exp_count, done)

    parts = seq_count // 2
    mine = opened(0)
    arrived, mine = lax.optimization_barrier((arrived, mine))
    done = None
    for part in range(parts):
        following = opened(part + 1) if part + 1 < parts else None
        done = closed(part, mine, done)
        arrived, done = lax.optimization_barrier((arrived, done))
        mine = following
    attn, done = lax.optimization_barrier((attn, done))
    attn = home(attn)
    back = exchange(done.reshape(devices, SLOTS, width // 2), all_axes)
    back = back.reshape(experts, 2, SLOTS, width // 2)
    chip = (lax.axis_index("seq") // 2)[None].astype(jnp.int32)
    out = combine(chip, back, own, attn, residual_in[0], cached_moe[0])
    return out[None]


def solution(mesh):
    return jax.shard_map(
        per_device,
        mesh=mesh,
        in_specs=(
            P("exp", "seq", None),
            P("exp", "seq", None),
            P("exp", "seq", None),
            P("exp", "seq", None),
            P("exp", "seq", None),
            P(),
            P("exp", "seq"),
            P("exp", "seq", None),
            P("exp", "seq", None),
            P(("seq", "exp"), None, None),
            P(("seq", "exp"), None, None),
            P(("seq", "exp"), None, None),
        ),
        out_specs=P("exp", "seq", None),
        check_vma=False,
    )
```

```python
import functools
import math

import jax
import jax.numpy as jnp
from jax import lax
from jax.experimental import pallas as pl
from jax.experimental.pallas import tpu as pltpu
from jax.sharding import PartitionSpec as P

HEAD_DIM = 128
TOP = 8
SLOTS = 8
bf16 = jnp.bfloat16
f32 = jnp.float32


def params(mib):
    return pltpu.CompilerParams(vmem_limit_bytes=mib * 1024 * 1024)


def iota(shape, dim):
    return lax.broadcasted_iota(jnp.int32, shape, dim)


def ones(where):
    return jnp.where(where, jnp.float32(1.0), jnp.float32(0.0)).astype(bf16)


def dot(a, b, dims=((1,), (0,))):
    return lax.dot_general(a, b, (dims, ((), ())), preferred_element_type=f32)


def half_kernel(half_ref, down_ref, out_ref):
    del half_ref
    out_ref[...] = down_ref[...]


def take_half(half, down):
    depth, width = down.shape
    steps = 4
    span = width // 2 // steps
    return pl.pallas_call(
        half_kernel,
        grid_spec=pltpu.PrefetchScalarGridSpec(
            num_scalar_prefetch=1,
            grid=(steps,),
            in_specs=[pl.BlockSpec((depth, span), lambda c, half: (0, half[0] * steps + c))],
            out_specs=pl.BlockSpec((depth, span), lambda c, half: (0, c)),
        ),
        out_shape=jax.ShapeDtypeStruct((depth, width // 2), bf16),
        compiler_params=params(60),
        name="take_half",
    )(half, down)


def prepare_kernel(
    q_ref,
    k_ref,
    v_ref,
    res_ref,
    flag_ref,
    ids_ref,
    gates_ref,
    out_ref,
    own_ref,
    pick_ref,
    table_ref,
):
    rows = q_ref.shape[0]
    merge, _, cols = out_ref.shape
    experts, most = table_ref.shape
    extra = 3 * rows + most

    @pl.when(pl.program_id(0) == 0)
    def _():
        upper = ones(iota((rows, rows), 0) < iota((rows, rows), 1))
        masked = flag_ref[...] == 1
        rank = dot(ones(jnp.broadcast_to(flag_ref[...], (16, rows)) == 1), upper)[:1]
        pick = ones((iota((most, rows), 0).astype(f32) == rank) & masked)
        pick_ref[...] = pick
        slow = iota((experts, rows), 0)
        order = slow % TOP * TOP + slow // TOP
        named = jnp.zeros((experts, rows), f32)
        gates = jnp.zeros((experts, rows), f32)
        for k in range(TOP):
            hit = (order == ids_ref[k : k + 1, :]) & masked
            named = jnp.where(hit, 1.0, named)
            gates = jnp.where(hit, gates_ref[k : k + 1, :], gates)
        place = (named * (dot(named.astype(bf16), upper) + 1.0)).astype(bf16)
        high = gates.astype(bf16)
        own_ref[0] = place
        own_ref[1] = high
        own_ref[2] = (gates - high.astype(f32)).astype(bf16)
        table_ref[...] = dot(place, pick, ((1,), (1,))).astype(bf16)

    numbers = iota((16, rows), 1).astype(f32).astype(bf16)
    spot = dot(numbers, pick_ref[...], ((1,), (1,)))
    count = dot(jnp.ones((16, rows), bf16), pick_ref[...], ((1,), (1,)))
    spot = jnp.where(count > 0.5, spot, -1.0).astype(bf16)
    for m in range(merge):
        here = slice(m * cols, (m + 1) * cols)
        out_ref[m, :rows] = q_ref[:, here]
        out_ref[m, rows : 2 * rows] = k_ref[:, here]
        out_ref[m, 2 * rows : 3 * rows] = v_ref[:, here]
        out_ref[m, 3 * rows : extra] = dot(pick_ref[...], res_ref[:, here]).astype(bf16)
        out_ref[m, extra:] = jnp.zeros((16, cols), bf16)
        for h in range(experts // 16):
            out_ref[m, extra:, h * 128 : h * 128 + most] = table_ref[h * 16 : (h + 1) * 16]
            out_ref[m, extra:, h * 128 + 64 : h * 128 + 64 + most] = spot


def prepare(q, k, v, res, flags, ids, gates, groups, experts, most):
    rows, width = q.shape
    cols = width // groups
    total = 3 * rows + most + 16
    merge = 2
    piece = pl.BlockSpec((rows, merge * cols), lambda j: (0, j))
    return pl.pallas_call(
        prepare_kernel,
        grid=(groups // merge,),
        in_specs=[
            piece,
            piece,
            piece,
            piece,
            pl.BlockSpec((1, rows), lambda j: (0, 0)),
            pl.BlockSpec((TOP, rows), lambda j: (0, 0)),
            pl.BlockSpec((TOP, rows), lambda j: (0, 0)),
        ],
        out_specs=[
            pl.BlockSpec((merge, total, cols), lambda j: (j, 0, 0)),
            pl.BlockSpec((3, experts, rows), lambda j: (0, 0, 0)),
        ],
        out_shape=[
            jax.ShapeDtypeStruct((groups, total, cols), bf16),
            jax.ShapeDtypeStruct((3, experts, rows), bf16),
        ],
        scratch_shapes=[pltpu.VMEM((most, rows), bf16), pltpu.VMEM((experts, most), bf16)],
        compiler_params=params(60),
        name="prepare",
    )(q, k, v, res, flags, ids, gates)


def attend_kernel(in_ref, attn_ref, v_ref):
    blocks, rows, cols = attn_ref.shape
    length = blocks * rows
    scale = math.log2(math.e) / math.sqrt(HEAD_DIM)
    step = 2
    v_ref[:, HEAD_DIM:] = jnp.ones((length, HEAD_DIM), bf16)
    for h in range(cols // HEAD_DIM):
        here = slice(h * HEAD_DIM, (h + 1) * HEAD_DIM)
        k_all = in_ref[:, rows : 2 * rows, here].reshape(length, HEAD_DIM)
        v_ref[:, :HEAD_DIM] = in_ref[:, 2 * rows : 3 * rows, here].reshape(length, HEAD_DIM)
        for first in range(0, blocks, step):
            q_part = in_ref[first : first + step, :rows, here].reshape(step * rows, HEAD_DIM)
            scores = dot(q_part, k_all, ((1,), (1,)))
            peak = jnp.max(scores, axis=-1, keepdims=True)
            expo = jnp.exp2((scores - peak) * scale).astype(bf16)
            mixed = dot(expo, v_ref[...])
            attn = (mixed[:, :HEAD_DIM] / mixed[:, HEAD_DIM:]).astype(bf16)
            attn_ref[first : first + step, :, here] = attn.reshape(step, rows, HEAD_DIM)


def attend(pieces, rows, heads=2):
    blocks, _, cols = pieces.shape
    span = heads * HEAD_DIM
    return pl.pallas_call(
        attend_kernel,
        grid=(cols // span,),
        in_specs=[pl.BlockSpec((blocks, 3 * rows, span), lambda h: (0, 0, h))],
        out_specs=pl.BlockSpec((blocks, rows, span), lambda h: (0, 0, h)),
        out_shape=jax.ShapeDtypeStruct((blocks, rows, cols), bf16),
        scratch_shapes=[pltpu.VMEM((blocks * rows, 2 * HEAD_DIM), bf16)],
        compiler_params=params(60),
        name="attend",
    )(pieces)


def pick_kernel(attn_ref, res_ref, table_ref, gain_ref, out_ref, place_ref, spot_ref):
    blocks, rows, cols = attn_ref.shape
    experts, most = place_ref.shape[1] // SLOTS, place_ref.shape[2]

    @pl.when(pl.program_id(0) == 0)
    def _():
        wanted = iota((16, SLOTS, most), 1).astype(f32) + 1.0
        for b in range(blocks):
            for h in range(experts // 16):
                table = table_ref[b, :, h * 128 : h * 128 + most].astype(f32)
                hit = jnp.where(table[:, None, :] == wanted, 1.0, 0.0)
                place_ref[b, h * 128 : (h + 1) * 128] = hit.reshape(128, most).astype(bf16)
            spot = table_ref[b, :, 64 : 64 + most].astype(f32)[:1]
            spot_ref[b] = ones(iota((rows, most), 0).astype(f32) == spot)

    gain = gain_ref[...].astype(f32)
    for b in range(blocks):
        hidden = dot(spot_ref[b], attn_ref[b], ((0,), (0,))) + res_ref[b].astype(f32)
        sent = dot(place_ref[b], (hidden * gain).astype(bf16))
        sent = sent.reshape(TOP, experts // TOP, SLOTS, cols).astype(bf16)
        out_ref[:, 0, :, b] = sent
        out_ref[:, 1, :, b] = sent


def pick(attn, pieces, gain, experts):
    blocks, rows, cols = attn.shape
    total = pieces.shape[1]
    most = total - 3 * rows - 16
    span = 256
    blocked = experts // TOP
    return pl.pallas_call(
        pick_kernel,
        grid=(cols // span,),
        in_specs=[
            pl.BlockSpec((blocks, rows, span), lambda h: (0, 0, h)),
            pl.BlockSpec((blocks, most, span), lambda h: (0, 3 * rows // most, h)),
            pl.BlockSpec((blocks, 16, cols), lambda h: (0, total // 16 - 1, 0)),
            pl.BlockSpec((1, span), lambda h: (0, h)),
        ],
        out_specs=pl.BlockSpec(
            (TOP, 2, blocked, blocks, SLOTS, span), lambda h: (0, 0, 0, 0, 0, h)
        ),
        out_shape=jax.ShapeDtypeStruct((TOP, 2, blocked, blocks, SLOTS, cols), bf16),
        scratch_shapes=[
            pltpu.VMEM((blocks, experts * SLOTS, most), bf16),
            pltpu.VMEM((blocks, rows, most), bf16),
        ],
        compiler_params=params(60),
        name="pick",
    )(attn, pieces, pieces, gain)


def open_kernel(
    rows_ref, weigh_ref, gate_ref, up_ref, out_ref, gates_ref, ups_ref, square_ref
):
    step = pl.program_id(0)
    last = pl.num_programs(0) - 1
    count, merge, per, cols = rows_ref.shape
    total = count * per

    @pl.when(step == 0)
    def _():
        gates_ref[...] = jnp.zeros_like(gates_ref)
        ups_ref[...] = jnp.zeros_like(ups_ref)
        square_ref[...] = jnp.zeros_like(square_ref)

    tiles = max(total // 256, 1)
    tile = total // tiles
    for t in range(tiles):
        inside = slice(t * count // tiles, (t + 1) * count // tiles)
        rows = slice(t * tile, (t + 1) * tile)
        gate_part = gates_ref[rows]
        up_part = ups_ref[rows]
        square = square_ref[rows]
        for m in range(merge):
            here = slice(m * cols, (m + 1) * cols)
            x = rows_ref[inside, m].reshape(tile, cols)
            gate_part += dot(x, gate_ref[here])
            up_part += dot(x, up_ref[here])
            square += dot(x * x, weigh_ref[here])
        gates_ref[rows] = gate_part
        ups_ref[rows] = up_part
        square_ref[rows] = square

    @pl.when(step == last)
    def _():
        mean = (square_ref[:, :1] + square_ref[:, 1:2]) / ((last + 1) * merge * cols)
        scale = lax.rsqrt(mean + 1e-06)
        gate_full = gates_ref[...] * scale
        act = gate_full / (1.0 + jnp.exp(-gate_full)) * (ups_ref[...] * scale)
        out_ref[...] = act.astype(bf16)


def expert_open(arrived, part, per, weigh, gate, up):
    count, groups, _, cols = arrived.shape
    width, half = gate.shape
    total = count * per
    merge = 2
    weight = pl.BlockSpec((merge * cols, half), lambda n: (n, 0))
    return pl.pallas_call(
        open_kernel,
        grid=(groups // merge,),
        in_specs=[
            pl.BlockSpec((count, merge, per, cols), lambda n: (0, n, part, 0)),
            pl.BlockSpec((merge * cols, 128), lambda n: (n, 0)),
            weight,
            weight,
        ],
        out_specs=pl.BlockSpec((total, half), lambda n: (0, 0)),
        out_shape=jax.ShapeDtypeStruct((total, half), bf16),
        scratch_shapes=[
            pltpu.VMEM((total, half), f32),
            pltpu.VMEM((total, half), f32),
            pltpu.VMEM((total, 128), f32),
        ],
        compiler_params=params(52),
        cost_estimate=pl.CostEstimate(
            flops=4 * total * width * half,
            bytes_accessed=4 * width * half + 2 * total * (width + half),
            transcendentals=total * half,
        ),
        name="expert_open",
    )(arrived, weigh, gate, up)


def close_kernel(
    role_ref, first_ref, mine_ref, second_ref, first_down, own_down, second_down, *rest
):
    out_ref = rest[-1]
    def emit(act_ref, down_ref):
        result = dot(first_ref[...], first_down[...]) + dot(act_ref[...], down_ref[...])
        out_ref[...] = result.reshape(out_ref.shape).astype(bf16)

    @pl.when(role_ref[0] == 1)
    def _():
        emit(mine_ref, own_down)

    @pl.when(role_ref[0] == 0)
    def _():
        emit(second_ref, second_down)


def expert_close(role, acts, downs, part, groups, count, done):
    total, half = acts[0].shape
    width = downs[0].shape[1]
    span = 512
    steps = width // span
    merge = total // (count * SLOTS)
    act = pl.BlockSpec((total, half), lambda c, role: (0, 0))
    held = [] if done is None else [done]

    def down(place):
        return pl.BlockSpec((half, span), lambda c, role: (0, place(c, role)))

    return pl.pallas_call(
        close_kernel,
        grid_spec=pltpu.PrefetchScalarGridSpec(
            num_scalar_prefetch=1,
            grid=(steps,),
            in_specs=[
                act,
                act,
                act,
                down(lambda c, role: c),
                down(lambda c, role: role[0] * (role[1] * steps + c)),
                down(lambda c, role: (1 - role[0]) * c),
            ]
            + [pl.BlockSpec(memory_space=pl.ANY)] * len(held),
            out_specs=pl.BlockSpec((count, merge, SLOTS, span), lambda c, role: (0, part, 0, c)),
        ),
        out_shape=jax.ShapeDtypeStruct((count, groups, SLOTS, width), bf16),
        input_output_aliases={7: 0} if held else {},
        compiler_params=params(44),
        cost_estimate=pl.CostEstimate(
            flops=4 * total * width * half,
            bytes_accessed=2 * (2 * width * half + total * (2 * half + width)),
            transcendentals=0,
        ),
        name="expert_close",
    )(role, *acts, *downs, *held)


def combine_kernel(back_ref, own_ref, attn_ref, res_ref, cached_ref, out_ref, mix_ref):
    _, experts, rows = own_ref.shape
    slots = experts * SLOTS
    cols = out_ref.shape[1]

    @pl.when(pl.program_id(0) == 0)
    def _():
        column = iota((experts, slots), 1) // SLOTS
        order = column // 8 * 8 + column % 4 * 2 + column // 4 % 2
        spread = ones(iota((experts, slots), 0) == order)
        slot = (iota((rows, slots), 1) % SLOTS + 1).astype(f32)
        hit = dot(own_ref[0], spread, ((0,), (0,))) == slot
        for i in range(2):
            gates = dot(own_ref[1 + i], spread, ((0,), (0,)))
            mix_ref[i * rows : (i + 1) * rows] = jnp.where(hit, gates, 0.0).astype(bf16)

    both = dot(mix_ref[...], back_ref[...].reshape(slots, cols))
    mixed = both[:rows] + both[rows:]
    named = dot(own_ref[0], jnp.ones((experts, 128), bf16), ((0,), (0,)))
    moe = jnp.where(named[:, :1] > 0.5, mixed, cached_ref[...].astype(f32))
    merge, _, piece = attn_ref.shape
    for m in range(merge):
        here = slice(m * piece, (m + 1) * piece)
        hid = res_ref[:, here].astype(f32) + attn_ref[m].astype(f32)
        out_ref[:, here] = (hid + moe[:, here]).astype(bf16)


def combine(back, own, attn, residual, cached, span=1024):
    count, chips, cores, _, half = back.shape
    groups, rows, piece = attn.shape
    width = groups * piece
    experts = own.shape[1]
    merge = span // piece
    steps = half // span
    flat = pl.BlockSpec((rows, span), lambda j: (0, j))
    return pl.pallas_call(
        combine_kernel,
        grid=(width // span,),
        in_specs=[
            pl.BlockSpec(
                (count, chips, 1, SLOTS, span), lambda j: (0, 0, j // steps, 0, j % steps)
            ),
            pl.BlockSpec(own.shape, lambda j: (0, 0, 0)),
            pl.BlockSpec((merge, rows, piece), lambda j: (j, 0, 0)),
            flat,
            flat,
        ],
        out_specs=flat,
        out_shape=jax.ShapeDtypeStruct((rows, width), bf16),
        scratch_shapes=[pltpu.VMEM((2 * rows, experts * SLOTS), bf16)],
        compiler_params=params(60),
        name="combine",
    )(back, own, attn, residual, cached)


def exchange(blocks, axes):
    return lax.all_to_all(blocks, axes, split_axis=0, concat_axis=0, tiled=True)


def per_device(
    queries,
    keys,
    values,
    residual_in,
    cached_moe,
    norm_gain,
    still_masked,
    expert_ids,
    gate_weights,
    w_gate,
    w_up,
    w_down,
):
    rows, width = queries.shape[1:]
    seq_count = lax.axis_size("seq")
    exp_count = lax.axis_size("exp")
    devices = seq_count * exp_count
    experts = devices // 2
    cols = width // seq_count
    most = rows * 3 // 8
    all_axes = ("seq", "exp")
    gain = norm_gain[None, :]
    own_gain = lax.dynamic_slice_in_dim(gain, lax.axis_index("seq") * cols, cols, 1)
    weigh = 1.0 / jnp.square(norm_gain.astype(f32))
    high = weigh.astype(bf16)
    low = (weigh - high.astype(f32)).astype(bf16)
    weigh = jnp.pad(jnp.stack([high, low], axis=1), ((0, 0), (0, 126)))

    ring, cross, beside = [], [], []
    for s in range(seq_count):
        for p in range(exp_count):
            here = s * exp_count + p
            other_core = (s ^ 1) * exp_count + p
            other_chip = s * exp_count + (p ^ 1)
            both = (s ^ 1) * exp_count + (p ^ 1)
            if p % 2 == s % 2:
                ring.append((here, other_core))
                beside.append((here, other_core))
            else:
                ring.append((here, other_chip))
                cross.append((here, both))
    core = lax.axis_index("seq") % 2
    odd = lax.axis_index("exp") % 2
    role = jnp.stack([(core == odd).astype(jnp.int32), core.astype(jnp.int32)])

    first_down = take_half((1 - odd)[None].astype(jnp.int32), w_down[0])
    first_down = lax.ppermute(first_down, all_axes, ring)
    second_down = take_half(odd[None].astype(jnp.int32), w_down[0])
    second_down = lax.ppermute(second_down, all_axes, cross)
    pieces, own = prepare(
        queries[0],
        keys[0],
        values[0],
        residual_in[0],
        still_masked,
        expert_ids[0].T,
        gate_weights[0].T,
        seq_count,
        experts,
        most,
    )
    pieces = exchange(pieces, "seq")
    tied = lax.optimization_barrier((pieces, weigh, own_gain, first_down))
    pieces, weigh, own_gain, first_down = tied

    attn = attend(pieces, rows)
    sent = pick(attn, pieces, own_gain, experts)
    attn = exchange(attn, "seq")
    sent, attn, second_down = lax.optimization_barrier((sent, attn, second_down))
    arrived = exchange(sent.reshape(devices, seq_count * SLOTS, cols), ("exp", "seq"))
    arrived = arrived.reshape(exp_count, seq_count, seq_count * SLOTS, cols)

    parts = 2
    per = seq_count * SLOTS // parts
    mine, first = [], []
    for part in range(parts):
        mine.append(expert_open(arrived, part, per, weigh, w_gate[0], w_up[0]))
        arrived, mine[part] = lax.optimization_barrier((arrived, mine[part]))
        first.append(lax.ppermute(mine[part], all_axes, ring))
    first[0], mine[1] = lax.optimization_barrier((first[0], mine[1]))
    downs = (first_down, w_down[0], second_down)
    done = None
    for part in range(parts):
        second = lax.ppermute(first[part], all_axes, beside)
        acts = (first[part], mine[part], second)
        done = expert_close(role, acts, downs, part, seq_count, exp_count, done)
        if part == 0:
            first[1], done = lax.optimization_barrier((first[1], done))
    back = exchange(done.reshape(devices, SLOTS, width // 2), ("exp", "seq"))
    back = back.reshape(exp_count, seq_count // 2, 2, SLOTS, width // 2)
    out = combine(back, own, attn, residual_in[0], cached_moe[0])
    return out[None]


def solution(mesh):
    return jax.shard_map(
        per_device,
        mesh=mesh,
        in_specs=(
            P("exp", "seq", None),
            P("exp", "seq", None),
            P("exp", "seq", None),
            P("exp", "seq", None),
            P("exp", "seq", None),
            P(),
            P("exp", "seq"),
            P("exp", "seq", None),
            P("exp", "seq", None),
            P(("seq", "exp"), None, None),
            P(("seq", "exp"), None, None),
            P(("seq", "exp"), None, None),
        ),
        out_specs=P("exp", "seq", None),
        check_vma=False,
    )
```

```python
import functools
import math

import jax
import jax.numpy as jnp
from jax import lax
from jax.experimental import pallas as pl
from jax.experimental.pallas import tpu as pltpu
from jax.sharding import PartitionSpec as P

HEAD_DIM = 128
TOP = 8
SLOTS = 8
bf16 = jnp.bfloat16
f32 = jnp.float32


def params(mib):
    return pltpu.CompilerParams(vmem_limit_bytes=mib * 1024 * 1024)


def iota(shape, dim):
    return lax.broadcasted_iota(jnp.int32, shape, dim)


def ones(where):
    return jnp.where(where, jnp.float32(1.0), jnp.float32(0.0)).astype(bf16)


def dot(a, b, dims=((1,), (0,))):
    return lax.dot_general(a, b, (dims, ((), ())), preferred_element_type=f32)


def half_kernel(half_ref, down_ref, out_ref):
    del half_ref
    out_ref[...] = down_ref[...]


def take_half(half, down):
    depth, width = down.shape
    steps = 4
    span = width // 2 // steps
    return pl.pallas_call(
        half_kernel,
        grid_spec=pltpu.PrefetchScalarGridSpec(
            num_scalar_prefetch=1,
            grid=(steps,),
            in_specs=[pl.BlockSpec((depth, span), lambda c, half: (0, half[0] * steps + c))],
            out_specs=pl.BlockSpec((depth, span), lambda c, half: (0, c)),
        ),
        out_shape=jax.ShapeDtypeStruct((depth, width // 2), bf16),
        compiler_params=params(60),
        name="take_half",
    )(half, down)


def stage_kernel(gate_ref, up_ref, gate_out, up_out):
    gate_out[...] = gate_ref[...]
    up_out[...] = up_ref[...]


def stage(gate, up):
    width, depth = gate.shape
    steps = 8
    spec = pl.BlockSpec((width // steps, depth), lambda r: (r, 0))
    return pl.pallas_call(
        stage_kernel,
        grid=(steps,),
        in_specs=[spec, spec],
        out_specs=[spec, spec],
        out_shape=[
            jax.ShapeDtypeStruct(gate.shape, bf16),
            jax.ShapeDtypeStruct(up.shape, bf16),
        ],
        compiler_params=params(16),
        name="stage",
    )(gate, up)


def prepare_kernel(
    q_ref,
    k_ref,
    v_ref,
    res_ref,
    flag_ref,
    ids_ref,
    gates_ref,
    out_ref,
    own_ref,
    pick_ref,
    table_ref,
):
    rows = q_ref.shape[0]
    merge, _, cols = out_ref.shape
    experts, most = table_ref.shape
    extra = 3 * rows + most

    @pl.when(pl.program_id(0) == 0)
    def _():
        upper = ones(iota((rows, rows), 0) < iota((rows, rows), 1))
        masked = flag_ref[...] == 1
        rank = dot(ones(jnp.broadcast_to(flag_ref[...], (16, rows)) == 1), upper)[:1]
        pick = ones((iota((most, rows), 0).astype(f32) == rank) & masked)
        pick_ref[...] = pick
        slow = iota((experts, rows), 0)
        order = slow % TOP * TOP + slow // TOP
        named = jnp.zeros((experts, rows), f32)
        gates = jnp.zeros((experts, rows), f32)
        for k in range(TOP):
            hit = (order == ids_ref[k : k + 1, :]) & masked
            named = jnp.where(hit, 1.0, named)
            gates = jnp.where(hit, gates_ref[k : k + 1, :], gates)
        place = (named * (dot(named.astype(bf16), upper) + 1.0)).astype(bf16)
        high = gates.astype(bf16)
        own_ref[0] = place
        own_ref[1] = high
        own_ref[2] = (gates - high.astype(f32)).astype(bf16)
        table_ref[...] = dot(place, pick, ((1,), (1,))).astype(bf16)

    numbers = iota((16, rows), 1).astype(f32).astype(bf16)
    spot = dot(numbers, pick_ref[...], ((1,), (1,)))
    count = dot(jnp.ones((16, rows), bf16), pick_ref[...], ((1,), (1,)))
    spot = jnp.where(count > 0.5, spot, -1.0).astype(bf16)
    for m in range(merge):
        here = slice(m * cols, (m + 1) * cols)
        out_ref[m, :rows] = q_ref[:, here]
        out_ref[m, rows : 2 * rows] = k_ref[:, here]
        out_ref[m, 2 * rows : 3 * rows] = v_ref[:, here]
        out_ref[m, 3 * rows : extra] = dot(pick_ref[...], res_ref[:, here]).astype(bf16)
        out_ref[m, extra:] = jnp.zeros((16, cols), bf16)
        for h in range(experts // 16):
            out_ref[m, extra:, h * 128 : h * 128 + most] = table_ref[h * 16 : (h + 1) * 16]
            out_ref[m, extra:, h * 128 + 64 : h * 128 + 64 + most] = spot


def prepare(q, k, v, res, flags, ids, gates, groups, experts, most):
    rows, width = q.shape
    cols = width // groups
    total = 3 * rows + most + 16
    merge = 2
    piece = pl.BlockSpec((rows, merge * cols), lambda j: (0, j))
    return pl.pallas_call(
        prepare_kernel,
        grid=(groups // merge,),
        in_specs=[
            piece,
            piece,
            piece,
            piece,
            pl.BlockSpec((1, rows), lambda j: (0, 0)),
            pl.BlockSpec((TOP, rows), lambda j: (0, 0)),
            pl.BlockSpec((TOP, rows), lambda j: (0, 0)),
        ],
        out_specs=[
            pl.BlockSpec((merge, total, cols), lambda j: (j, 0, 0)),
            pl.BlockSpec((3, experts, rows), lambda j: (0, 0, 0)),
        ],
        out_shape=[
            jax.ShapeDtypeStruct((groups, total, cols), bf16),
            jax.ShapeDtypeStruct((3, experts, rows), bf16),
        ],
        scratch_shapes=[pltpu.VMEM((most, rows), bf16), pltpu.VMEM((experts, most), bf16)],
        compiler_params=params(60),
        name="prepare",
    )(q, k, v, res, flags, ids, gates)


def attend_kernel(in_ref, attn_ref, v_ref):
    blocks, rows, cols = attn_ref.shape
    length = blocks * rows
    scale = math.log2(math.e) / math.sqrt(HEAD_DIM)
    step = 2
    v_ref[:, HEAD_DIM:] = jnp.ones((length, HEAD_DIM), bf16)
    for h in range(cols // HEAD_DIM):
        here = slice(h * HEAD_DIM, (h + 1) * HEAD_DIM)
        k_all = in_ref[:, rows : 2 * rows, here].reshape(length, HEAD_DIM)
        v_ref[:, :HEAD_DIM] = in_ref[:, 2 * rows : 3 * rows, here].reshape(length, HEAD_DIM)
        for first in range(0, blocks, step):
            q_part = in_ref[first : first + step, :rows, here].reshape(step * rows, HEAD_DIM)
            scores = dot(q_part, k_all, ((1,), (1,)))
            peak = jnp.max(scores, axis=-1, keepdims=True)
            expo = jnp.exp2((scores - peak) * scale).astype(bf16)
            mixed = dot(expo, v_ref[...])
            attn = (mixed[:, :HEAD_DIM] / mixed[:, HEAD_DIM:]).astype(bf16)
            attn_ref[first : first + step, :, here] = attn.reshape(step, rows, HEAD_DIM)


def attend(pieces, rows, heads=2):
    blocks, _, cols = pieces.shape
    span = heads * HEAD_DIM
    return pl.pallas_call(
        attend_kernel,
        grid=(cols // span,),
        in_specs=[pl.BlockSpec((blocks, 3 * rows, span), lambda h: (0, 0, h))],
        out_specs=pl.BlockSpec((blocks, rows, span), lambda h: (0, 0, h)),
        out_shape=jax.ShapeDtypeStruct((blocks, rows, cols), bf16),
        scratch_shapes=[pltpu.VMEM((blocks * rows, 2 * HEAD_DIM), bf16)],
        compiler_params=params(60),
        name="attend",
    )(pieces)


def pick_kernel(attn_ref, res_ref, table_ref, gain_ref, out_ref, place_ref, spot_ref):
    blocks, rows, cols = attn_ref.shape
    experts, most = place_ref.shape[1] // SLOTS, place_ref.shape[2]

    @pl.when(pl.program_id(0) == 0)
    def _():
        wanted = iota((16, SLOTS, most), 1).astype(f32) + 1.0
        for b in range(blocks):
            for h in range(experts // 16):
                table = table_ref[b, :, h * 128 : h * 128 + most].astype(f32)
                hit = jnp.where(table[:, None, :] == wanted, 1.0, 0.0)
                place_ref[b, h * 128 : (h + 1) * 128] = hit.reshape(128, most).astype(bf16)
            spot = table_ref[b, :, 64 : 64 + most].astype(f32)[:1]
            spot_ref[b] = ones(iota((rows, most), 0).astype(f32) == spot)

    gain = gain_ref[...].astype(f32)
    for b in range(blocks):
        hidden = dot(spot_ref[b], attn_ref[b], ((0,), (0,))) + res_ref[b].astype(f32)
        sent = dot(place_ref[b], (hidden * gain).astype(bf16))
        sent = sent.reshape(TOP, experts // TOP, SLOTS, cols).astype(bf16)
        out_ref[:, 0, :, b] = sent
        out_ref[:, 1, :, b] = sent


def pick(attn, pieces, gain, experts):
    blocks, rows, cols = attn.shape
    total = pieces.shape[1]
    most = total - 3 * rows - 16
    span = 256
    blocked = experts // TOP
    return pl.pallas_call(
        pick_kernel,
        grid=(cols // span,),
        in_specs=[
            pl.BlockSpec((blocks, rows, span), lambda h: (0, 0, h)),
            pl.BlockSpec((blocks, most, span), lambda h: (0, 3 * rows // most, h)),
            pl.BlockSpec((blocks, 16, cols), lambda h: (0, total // 16 - 1, 0)),
            pl.BlockSpec((1, span), lambda h: (0, h)),
        ],
        out_specs=pl.BlockSpec(
            (TOP, 2, blocked, blocks, SLOTS, span), lambda h: (0, 0, 0, 0, 0, h)
        ),
        out_shape=jax.ShapeDtypeStruct((TOP, 2, blocked, blocks, SLOTS, cols), bf16),
        scratch_shapes=[
            pltpu.VMEM((blocks, experts * SLOTS, most), bf16),
            pltpu.VMEM((blocks, rows, most), bf16),
        ],
        compiler_params=params(60),
        name="pick",
    )(attn, pieces, pieces, gain)


def open_kernel(
    rows_ref, weigh_ref, gate_ref, up_ref, out_ref, gates_ref, ups_ref, square_ref
):
    step = pl.program_id(0)
    last = pl.num_programs(0) - 1
    count, merge, per, cols = rows_ref.shape
    total = count * per

    @pl.when(step == 0)
    def _():
        gates_ref[...] = jnp.zeros_like(gates_ref)
        ups_ref[...] = jnp.zeros_like(ups_ref)
        square_ref[...] = jnp.zeros_like(square_ref)

    tiles = max(total // 256, 1)
    tile = total // tiles
    for t in range(tiles):
        inside = slice(t * count // tiles, (t + 1) * count // tiles)
        rows = slice(t * tile, (t + 1) * tile)
        gate_part = gates_ref[rows]
        up_part = ups_ref[rows]
        square = square_ref[rows]
        for m in range(merge):
            here = slice(m * cols, (m + 1) * cols)
            x = rows_ref[inside, m].reshape(tile, cols)
            gate_part += dot(x, gate_ref[here])
            up_part += dot(x, up_ref[here])
            square += dot(x * x, weigh_ref[here])
        gates_ref[rows] = gate_part
        ups_ref[rows] = up_part
        square_ref[rows] = square

    @pl.when(step == last)
    def _():
        mean = (square_ref[:, :1] + square_ref[:, 1:2]) / ((last + 1) * merge * cols)
        scale = lax.rsqrt(mean + 1e-06)
        gate_full = gates_ref[...] * scale
        act = gate_full / (1.0 + jnp.exp(-gate_full)) * (ups_ref[...] * scale)
        out_ref[...] = act.astype(bf16)


def expert_open(arrived, part, per, weigh, gate, up):
    count, groups, _, cols = arrived.shape
    width, half = gate.shape
    total = count * per
    merge = 2
    weight = pl.BlockSpec((merge * cols, half), lambda n: (n, 0))
    return pl.pallas_call(
        open_kernel,
        grid=(groups // merge,),
        in_specs=[
            pl.BlockSpec((count, merge, per, cols), lambda n: (0, n, part, 0)),
            pl.BlockSpec((merge * cols, 128), lambda n: (n, 0)),
            weight,
            weight,
        ],
        out_specs=pl.BlockSpec((total, half), lambda n: (0, 0)),
        out_shape=jax.ShapeDtypeStruct((total, half), bf16),
        scratch_shapes=[
            pltpu.VMEM((total, half), f32),
            pltpu.VMEM((total, half), f32),
            pltpu.VMEM((total, 128), f32),
        ],
        compiler_params=params(26),
        cost_estimate=pl.CostEstimate(
            flops=4 * total * width * half,
            bytes_accessed=4 * width * half + 2 * total * (width + half),
            transcendentals=total * half,
        ),
        name="expert_open",
    )(arrived, weigh, gate, up)


def close_kernel(
    role_ref, first_ref, mine_ref, second_ref, first_down, own_down, second_down, *rest
):
    out_ref = rest[-1]
    def emit(act_ref, down_ref):
        result = dot(first_ref[...], first_down[...]) + dot(act_ref[...], down_ref[...])
        out_ref[...] = result.reshape(out_ref.shape).astype(bf16)

    @pl.when(role_ref[0] == 1)
    def _():
        emit(mine_ref, own_down)

    @pl.when(role_ref[0] == 0)
    def _():
        emit(second_ref, second_down)


def expert_close(role, acts, downs, part, groups, count, done):
    total, half = acts[0].shape
    width = downs[0].shape[1]
    span = 512
    steps = width // span
    merge = total // (count * SLOTS)
    act = pl.BlockSpec((total, half), lambda c, role: (0, 0))
    held = [] if done is None else [done]

    def down(place):
        return pl.BlockSpec((half, span), lambda c, role: (0, place(c, role)))

    return pl.pallas_call(
        close_kernel,
        grid_spec=pltpu.PrefetchScalarGridSpec(
            num_scalar_prefetch=1,
            grid=(steps,),
            in_specs=[
                act,
                act,
                act,
                down(lambda c, role: c),
                down(lambda c, role: role[0] * (role[1] * steps + c)),
                down(lambda c, role: (1 - role[0]) * c),
            ]
            + [pl.BlockSpec(memory_space=pl.ANY)] * len(held),
            out_specs=pl.BlockSpec((count, merge, SLOTS, span), lambda c, role: (0, part, 0, c)),
        ),
        out_shape=jax.ShapeDtypeStruct((count, groups, SLOTS, width), bf16),
        input_output_aliases={7: 0} if held else {},
        compiler_params=params(44),
        cost_estimate=pl.CostEstimate(
            flops=4 * total * width * half,
            bytes_accessed=2 * (2 * width * half + total * (2 * half + width)),
            transcendentals=0,
        ),
        name="expert_close",
    )(role, *acts, *downs, *held)


def combine_kernel(back_ref, own_ref, attn_ref, res_ref, cached_ref, out_ref, mix_ref):
    _, experts, rows = own_ref.shape
    slots = experts * SLOTS
    cols = out_ref.shape[1]

    @pl.when(pl.program_id(0) == 0)
    def _():
        column = iota((experts, slots), 1) // SLOTS
        order = column // 8 * 8 + column % 4 * 2 + column // 4 % 2
        spread = ones(iota((experts, slots), 0) == order)
        slot = (iota((rows, slots), 1) % SLOTS + 1).astype(f32)
        hit = dot(own_ref[0], spread, ((0,), (0,))) == slot
        for i in range(2):
            gates = dot(own_ref[1 + i], spread, ((0,), (0,)))
            mix_ref[i * rows : (i + 1) * rows] = jnp.where(hit, gates, 0.0).astype(bf16)

    both = dot(mix_ref[...], back_ref[...].reshape(slots, cols))
    mixed = both[:rows] + both[rows:]
    named = dot(own_ref[0], jnp.ones((experts, 128), bf16), ((0,), (0,)))
    moe = jnp.where(named[:, :1] > 0.5, mixed, cached_ref[...].astype(f32))
    merge, _, piece = attn_ref.shape
    for m in range(merge):
        here = slice(m * piece, (m + 1) * piece)
        hid = res_ref[:, here].astype(f32) + attn_ref[m].astype(f32)
        out_ref[:, here] = (hid + moe[:, here]).astype(bf16)


def combine(back, own, attn, residual, cached, span=1024):
    count, chips, cores, _, half = back.shape
    groups, rows, piece = attn.shape
    width = groups * piece
    experts = own.shape[1]
    merge = span // piece
    steps = half // span
    flat = pl.BlockSpec((rows, span), lambda j: (0, j))
    return pl.pallas_call(
        combine_kernel,
        grid=(width // span,),
        in_specs=[
            pl.BlockSpec(
                (count, chips, 1, SLOTS, span), lambda j: (0, 0, j // steps, 0, j % steps)
            ),
            pl.BlockSpec(own.shape, lambda j: (0, 0, 0)),
            pl.BlockSpec((merge, rows, piece), lambda j: (j, 0, 0)),
            flat,
            flat,
        ],
        out_specs=flat,
        out_shape=jax.ShapeDtypeStruct((rows, width), bf16),
        scratch_shapes=[pltpu.VMEM((2 * rows, experts * SLOTS), bf16)],
        compiler_params=params(30),
        name="combine",
    )(back, own, attn, residual, cached)


def exchange(blocks, axes):
    return lax.all_to_all(blocks, axes, split_axis=0, concat_axis=0, tiled=True)


def per_device(
    queries,
    keys,
    values,
    residual_in,
    cached_moe,
    norm_gain,
    still_masked,
    expert_ids,
    gate_weights,
    w_gate,
    w_up,
    w_down,
):
    rows, width = queries.shape[1:]
    seq_count = lax.axis_size("seq")
    exp_count = lax.axis_size("exp")
    devices = seq_count * exp_count
    experts = devices // 2
    cols = width // seq_count
    most = rows * 3 // 8
    all_axes = ("seq", "exp")
    gain = norm_gain[None, :]
    own_gain = lax.dynamic_slice_in_dim(gain, lax.axis_index("seq") * cols, cols, 1)
    weigh = 1.0 / jnp.square(norm_gain.astype(f32))
    high = weigh.astype(bf16)
    low = (weigh - high.astype(f32)).astype(bf16)
    weigh = jnp.pad(jnp.stack([high, low], axis=1), ((0, 0), (0, 126)))

    ring, cross, beside = [], [], []
    for s in range(seq_count):
        for p in range(exp_count):
            here = s * exp_count + p
            other_core = (s ^ 1) * exp_count + p
            other_chip = s * exp_count + (p ^ 1)
            both = (s ^ 1) * exp_count + (p ^ 1)
            if p % 2 == s % 2:
                ring.append((here, other_core))
                beside.append((here, other_core))
            else:
                ring.append((here, other_chip))
                cross.append((here, both))
    core = lax.axis_index("seq") % 2
    odd = lax.axis_index("exp") % 2
    role = jnp.stack([(core == odd).astype(jnp.int32), core.astype(jnp.int32)])

    first_down = take_half((1 - odd)[None].astype(jnp.int32), w_down[0])
    first_down = lax.ppermute(first_down, all_axes, ring)
    second_down = take_half(odd[None].astype(jnp.int32), w_down[0])
    second_down = lax.ppermute(second_down, all_axes, cross)
    pieces, own = prepare(
        queries[0],
        keys[0],
        values[0],
        residual_in[0],
        still_masked,
        expert_ids[0].T,
        gate_weights[0].T,
        seq_count,
        experts,
        most,
    )
    pieces = exchange(pieces, "seq")
    tied = lax.optimization_barrier((pieces, weigh, own_gain, first_down))
    pieces, weigh, own_gain, first_down = tied

    attn = attend(pieces, rows)
    sent = pick(attn, pieces, own_gain, experts)
    attn = exchange(attn, "seq")
    gate, sent = lax.optimization_barrier((w_gate[0], sent))
    gate, up = stage(gate, w_up[0])
    tied = lax.optimization_barrier((sent, attn, second_down, gate, up))
    sent, attn, second_down, gate, up = tied
    arrived = exchange(sent.reshape(devices, seq_count * SLOTS, cols), ("exp", "seq"))
    arrived = arrived.reshape(exp_count, seq_count, seq_count * SLOTS, cols)

    parts = 2
    per = seq_count * SLOTS // parts
    mine, first = [], []
    for part in range(parts):
        mine.append(expert_open(arrived, part, per, weigh, gate, up))
        arrived, mine[part] = lax.optimization_barrier((arrived, mine[part]))
        first.append(lax.ppermute(mine[part], all_axes, ring))
    first[0], mine[1] = lax.optimization_barrier((first[0], mine[1]))
    downs = (first_down, w_down[0], second_down)
    done = None
    for part in range(parts):
        second = lax.ppermute(first[part], all_axes, beside)
        acts = (first[part], mine[part], second)
        done = expert_close(role, acts, downs, part, seq_count, exp_count, done)
        if part == 0:
            first[1], done = lax.optimization_barrier((first[1], done))
    back = exchange(done.reshape(devices, SLOTS, width // 2), ("exp", "seq"))
    back = back.reshape(exp_count, seq_count // 2, 2, SLOTS, width // 2)
    out = combine(back, own, attn, residual_in[0], cached_moe[0])
    return out[None]


def solution(mesh):
    return jax.shard_map(
        per_device,
        mesh=mesh,
        in_specs=(
            P("exp", "seq", None),
            P("exp", "seq", None),
            P("exp", "seq", None),
            P("exp", "seq", None),
            P("exp", "seq", None),
            P(),
            P("exp", "seq"),
            P("exp", "seq", None),
            P("exp", "seq", None),
            P(("seq", "exp"), None, None),
            P(("seq", "exp"), None, None),
            P(("seq", "exp"), None, None),
        ),
        out_specs=P("exp", "seq", None),
        check_vma=False,
    )
```

```python
import functools
import math

import jax
import jax.numpy as jnp
from jax import lax
from jax.experimental import pallas as pl
from jax.experimental.pallas import tpu as pltpu
from jax.sharding import PartitionSpec as P

HEAD_DIM = 128
TOP = 8
SLOTS = 8
bf16 = jnp.bfloat16
f32 = jnp.float32


def params(mib):
    return pltpu.CompilerParams(vmem_limit_bytes=mib * 1024 * 1024)


def iota(shape, dim):
    return lax.broadcasted_iota(jnp.int32, shape, dim)


def ones(where):
    return jnp.where(where, jnp.float32(1.0), jnp.float32(0.0)).astype(bf16)


def dot(a, b, dims=((1,), (0,))):
    return lax.dot_general(a, b, (dims, ((), ())), preferred_element_type=f32)


def half_kernel(half_ref, down_ref, out_ref):
    del half_ref
    out_ref[...] = down_ref[...]


def take_half(half, down):
    depth, width = down.shape
    steps = 4
    span = width // 2 // steps
    return pl.pallas_call(
        half_kernel,
        grid_spec=pltpu.PrefetchScalarGridSpec(
            num_scalar_prefetch=1,
            grid=(steps,),
            in_specs=[pl.BlockSpec((depth, span), lambda c, half: (0, half[0] * steps + c))],
            out_specs=pl.BlockSpec((depth, span), lambda c, half: (0, c)),
        ),
        out_shape=jax.ShapeDtypeStruct((depth, width // 2), bf16),
        compiler_params=params(60),
        name="take_half",
    )(half, down)


def stage_kernel(gate_ref, up_ref, gate_out, up_out):
    gate_out[...] = gate_ref[...]
    up_out[...] = up_ref[...]


def stage(gate, up):
    width, depth = gate.shape
    steps = 8
    spec = pl.BlockSpec((width // steps, depth), lambda r: (r, 0))
    return pl.pallas_call(
        stage_kernel,
        grid=(steps,),
        in_specs=[spec, spec],
        out_specs=[spec, spec],
        out_shape=[
            jax.ShapeDtypeStruct(gate.shape, bf16),
            jax.ShapeDtypeStruct(up.shape, bf16),
        ],
        compiler_params=params(16),
        name="stage",
    )(gate, up)


def prepare_kernel(
    q_ref,
    k_ref,
    v_ref,
    res_ref,
    flag_ref,
    ids_ref,
    gates_ref,
    out_ref,
    own_ref,
    pick_ref,
    table_ref,
):
    rows = q_ref.shape[0]
    merge, _, cols = out_ref.shape
    experts, most = table_ref.shape
    extra = 3 * rows + most

    @pl.when(pl.program_id(0) == 0)
    def _():
        upper = ones(iota((rows, rows), 0) < iota((rows, rows), 1))
        masked = flag_ref[...] == 1
        rank = dot(ones(jnp.broadcast_to(flag_ref[...], (16, rows)) == 1), upper)[:1]
        pick = ones((iota((most, rows), 0).astype(f32) == rank) & masked)
        pick_ref[...] = pick
        slow = iota((experts, rows), 0)
        order = slow % TOP * TOP + slow // TOP
        named = jnp.zeros((experts, rows), f32)
        gates = jnp.zeros((experts, rows), f32)
        for k in range(TOP):
            hit = (order == ids_ref[k : k + 1, :]) & masked
            named = jnp.where(hit, 1.0, named)
            gates = jnp.where(hit, gates_ref[k : k + 1, :], gates)
        place = (named * (dot(named.astype(bf16), upper) + 1.0)).astype(bf16)
        high = gates.astype(bf16)
        own_ref[0] = place
        own_ref[1] = high
        own_ref[2] = (gates - high.astype(f32)).astype(bf16)
        table_ref[...] = dot(place, pick, ((1,), (1,))).astype(bf16)

    numbers = iota((16, rows), 1).astype(f32).astype(bf16)
    spot = dot(numbers, pick_ref[...], ((1,), (1,)))
    count = dot(jnp.ones((16, rows), bf16), pick_ref[...], ((1,), (1,)))
    spot = jnp.where(count > 0.5, spot, -1.0).astype(bf16)
    for m in range(merge):
        here = slice(m * cols, (m + 1) * cols)
        out_ref[m, :rows] = q_ref[:, here]
        out_ref[m, rows : 2 * rows] = k_ref[:, here]
        out_ref[m, 2 * rows : 3 * rows] = v_ref[:, here]
        out_ref[m, 3 * rows : extra] = dot(pick_ref[...], res_ref[:, here]).astype(bf16)
        out_ref[m, extra:] = jnp.zeros((16, cols), bf16)
        for h in range(experts // 16):
            out_ref[m, extra:, h * 128 : h * 128 + most] = table_ref[h * 16 : (h + 1) * 16]
            out_ref[m, extra:, h * 128 + 64 : h * 128 + 64 + most] = spot


def prepare(q, k, v, res, flags, ids, gates, groups, experts, most):
    rows, width = q.shape
    cols = width // groups
    total = 3 * rows + most + 16
    merge = 2
    piece = pl.BlockSpec((rows, merge * cols), lambda j: (0, j))
    return pl.pallas_call(
        prepare_kernel,
        grid=(groups // merge,),
        in_specs=[
            piece,
            piece,
            piece,
            piece,
            pl.BlockSpec((1, rows), lambda j: (0, 0)),
            pl.BlockSpec((TOP, rows), lambda j: (0, 0)),
            pl.BlockSpec((TOP, rows), lambda j: (0, 0)),
        ],
        out_specs=[
            pl.BlockSpec((merge, total, cols), lambda j: (j, 0, 0)),
            pl.BlockSpec((3, experts, rows), lambda j: (0, 0, 0)),
        ],
        out_shape=[
            jax.ShapeDtypeStruct((groups, total, cols), bf16),
            jax.ShapeDtypeStruct((3, experts, rows), bf16),
        ],
        scratch_shapes=[pltpu.VMEM((most, rows), bf16), pltpu.VMEM((experts, most), bf16)],
        compiler_params=params(60),
        name="prepare",
    )(q, k, v, res, flags, ids, gates)


def attend_kernel(in_ref, attn_ref, v_ref):
    blocks, rows, cols = attn_ref.shape
    length = blocks * rows
    scale = math.log2(math.e) / math.sqrt(HEAD_DIM)
    step = 2
    v_ref[:, HEAD_DIM:] = jnp.ones((length, HEAD_DIM), bf16)
    for h in range(cols // HEAD_DIM):
        here = slice(h * HEAD_DIM, (h + 1) * HEAD_DIM)
        k_all = in_ref[:, rows : 2 * rows, here].reshape(length, HEAD_DIM)
        v_ref[:, :HEAD_DIM] = in_ref[:, 2 * rows : 3 * rows, here].reshape(length, HEAD_DIM)
        for first in range(0, blocks, step):
            q_part = in_ref[first : first + step, :rows, here].reshape(step * rows, HEAD_DIM)
            scores = dot(q_part, k_all, ((1,), (1,)))
            peak = jnp.max(scores, axis=-1, keepdims=True)
            expo = jnp.exp2((scores - peak) * scale).astype(bf16)
            mixed = dot(expo, v_ref[...])
            attn = (mixed[:, :HEAD_DIM] / mixed[:, HEAD_DIM:]).astype(bf16)
            attn_ref[first : first + step, :, here] = attn.reshape(step, rows, HEAD_DIM)


def attend(pieces, rows, heads=2):
    blocks, _, cols = pieces.shape
    span = heads * HEAD_DIM
    return pl.pallas_call(
        attend_kernel,
        grid=(cols // span,),
        in_specs=[pl.BlockSpec((blocks, 3 * rows, span), lambda h: (0, 0, h))],
        out_specs=pl.BlockSpec((blocks, rows, span), lambda h: (0, 0, h)),
        out_shape=jax.ShapeDtypeStruct((blocks, rows, cols), bf16),
        scratch_shapes=[pltpu.VMEM((blocks * rows, 2 * HEAD_DIM), bf16)],
        compiler_params=params(60),
        name="attend",
    )(pieces)


def pick_kernel(attn_ref, res_ref, table_ref, gain_ref, out_ref, place_ref, spot_ref):
    blocks, rows, cols = attn_ref.shape
    experts, most = place_ref.shape[1] // SLOTS, place_ref.shape[2]

    @pl.when(pl.program_id(0) == 0)
    def _():
        wanted = iota((16, SLOTS, most), 1).astype(f32) + 1.0
        for b in range(blocks):
            for h in range(experts // 16):
                table = table_ref[b, :, h * 128 : h * 128 + most].astype(f32)
                hit = jnp.where(table[:, None, :] == wanted, 1.0, 0.0)
                place_ref[b, h * 128 : (h + 1) * 128] = hit.reshape(128, most).astype(bf16)
            spot = table_ref[b, :, 64 : 64 + most].astype(f32)[:1]
            spot_ref[b] = ones(iota((rows, most), 0).astype(f32) == spot)

    gain = gain_ref[...].astype(f32)
    for b in range(blocks):
        hidden = dot(spot_ref[b], attn_ref[b], ((0,), (0,))) + res_ref[b].astype(f32)
        sent = dot(place_ref[b], (hidden * gain).astype(bf16))
        sent = sent.reshape(TOP, experts // TOP, SLOTS, cols).astype(bf16)
        out_ref[:, 0, :, b] = sent
        out_ref[:, 1, :, b] = sent


def pick(attn, pieces, gain, experts):
    blocks, rows, cols = attn.shape
    total = pieces.shape[1]
    most = total - 3 * rows - 16
    span = 256
    blocked = experts // TOP
    return pl.pallas_call(
        pick_kernel,
        grid=(cols // span,),
        in_specs=[
            pl.BlockSpec((blocks, rows, span), lambda h: (0, 0, h)),
            pl.BlockSpec((blocks, most, span), lambda h: (0, 3 * rows // most, h)),
            pl.BlockSpec((blocks, 16, cols), lambda h: (0, total // 16 - 1, 0)),
            pl.BlockSpec((1, span), lambda h: (0, h)),
        ],
        out_specs=pl.BlockSpec(
            (TOP, 2, blocked, blocks, SLOTS, span), lambda h: (0, 0, 0, 0, 0, h)
        ),
        out_shape=jax.ShapeDtypeStruct((TOP, 2, blocked, blocks, SLOTS, cols), bf16),
        scratch_shapes=[
            pltpu.VMEM((blocks, experts * SLOTS, most), bf16),
            pltpu.VMEM((blocks, rows, most), bf16),
        ],
        compiler_params=params(60),
        name="pick",
    )(attn, pieces, pieces, gain)


def open_kernel(
    rows_ref, weigh_ref, gate_ref, up_ref, out_ref, gates_ref, ups_ref, square_ref
):
    step = pl.program_id(0)
    last = pl.num_programs(0) - 1
    count, merge, per, cols = rows_ref.shape
    total = count * per

    @pl.when(step == 0)
    def _():
        gates_ref[...] = jnp.zeros_like(gates_ref)
        ups_ref[...] = jnp.zeros_like(ups_ref)
        square_ref[...] = jnp.zeros_like(square_ref)

    tiles = max(total // 256, 1)
    tile = total // tiles
    for t in range(tiles):
        inside = slice(t * count // tiles, (t + 1) * count // tiles)
        rows = slice(t * tile, (t + 1) * tile)
        gate_part = gates_ref[rows]
        up_part = ups_ref[rows]
        square = square_ref[rows]
        for m in range(merge):
            here = slice(m * cols, (m + 1) * cols)
            x = rows_ref[inside, m].reshape(tile, cols)
            gate_part += dot(x, gate_ref[here])
            up_part += dot(x, up_ref[here])
            square += dot(x * x, weigh_ref[here])
        gates_ref[rows] = gate_part
        ups_ref[rows] = up_part
        square_ref[rows] = square

    @pl.when(step == last)
    def _():
        mean = (square_ref[:, :1] + square_ref[:, 1:2]) / ((last + 1) * merge * cols)
        scale = lax.rsqrt(mean + 1e-06)
        gate_full = gates_ref[...] * scale
        act = gate_full / (1.0 + jnp.exp(-gate_full)) * (ups_ref[...] * scale)
        out_ref[...] = act.astype(bf16)


def expert_open(arrived, part, per, weigh, gate, up):
    count, groups, _, cols = arrived.shape
    width, half = gate.shape
    total = count * per
    merge = 2
    weight = pl.BlockSpec((merge * cols, half), lambda n: (n, 0))
    return pl.pallas_call(
        open_kernel,
        grid=(groups // merge,),
        in_specs=[
            pl.BlockSpec((count, merge, per, cols), lambda n: (0, n, part, 0)),
            pl.BlockSpec((merge * cols, 128), lambda n: (n, 0)),
            weight,
            weight,
        ],
        out_specs=pl.BlockSpec((total, half), lambda n: (0, 0)),
        out_shape=jax.ShapeDtypeStruct((total, half), bf16),
        scratch_shapes=[
            pltpu.VMEM((total, half), f32),
            pltpu.VMEM((total, half), f32),
            pltpu.VMEM((total, 128), f32),
        ],
        compiler_params=params(26),
        cost_estimate=pl.CostEstimate(
            flops=4 * total * width * half,
            bytes_accessed=4 * width * half + 2 * total * (width + half),
            transcendentals=total * half,
        ),
        name="expert_open",
    )(arrived, weigh, gate, up)


def close_kernel(
    role_ref, first_ref, mine_ref, second_ref, first_down, own_down, second_down, *rest
):
    out_ref = rest[-1]
    def emit(act_ref, down_ref):
        result = dot(first_ref[...], first_down[...]) + dot(act_ref[...], down_ref[...])
        out_ref[...] = result.reshape(out_ref.shape).astype(bf16)

    @pl.when(role_ref[0] == 1)
    def _():
        emit(mine_ref, own_down)

    @pl.when(role_ref[0] == 0)
    def _():
        emit(second_ref, second_down)


def expert_close(role, acts, downs, part, groups, count, done):
    total, half = acts[0].shape
    width = downs[0].shape[1]
    span = 1024
    steps = width // span
    merge = total // (count * SLOTS)
    act = pl.BlockSpec((total, half), lambda c, role: (0, 0))
    held = [] if done is None else [done]

    def down(place):
        return pl.BlockSpec((half, span), lambda c, role: (0, place(c, role)))

    return pl.pallas_call(
        close_kernel,
        grid_spec=pltpu.PrefetchScalarGridSpec(
            num_scalar_prefetch=1,
            grid=(steps,),
            in_specs=[
                act,
                act,
                act,
                down(lambda c, role: c),
                down(lambda c, role: role[0] * (role[1] * steps + c)),
                down(lambda c, role: (1 - role[0]) * c),
            ]
            + [pl.BlockSpec(memory_space=pl.ANY)] * len(held),
            out_specs=pl.BlockSpec((count, merge, SLOTS, span), lambda c, role: (0, part, 0, c)),
        ),
        out_shape=jax.ShapeDtypeStruct((count, groups, SLOTS, width), bf16),
        input_output_aliases={7: 0} if held else {},
        compiler_params=params(44),
        cost_estimate=pl.CostEstimate(
            flops=4 * total * width * half,
            bytes_accessed=2 * (2 * width * half + total * (2 * half + width)),
            transcendentals=0,
        ),
        name="expert_close",
    )(role, *acts, *downs, *held)


def combine_kernel(back_ref, own_ref, attn_ref, res_ref, cached_ref, out_ref, mix_ref):
    _, experts, rows = own_ref.shape
    slots = experts * SLOTS
    cols = out_ref.shape[1]

    @pl.when(pl.program_id(0) == 0)
    def _():
        column = iota((experts, slots), 1) // SLOTS
        order = column // 8 * 8 + column % 4 * 2 + column // 4 % 2
        spread = ones(iota((experts, slots), 0) == order)
        slot = (iota((rows, slots), 1) % SLOTS + 1).astype(f32)
        hit = dot(own_ref[0], spread, ((0,), (0,))) == slot
        for i in range(2):
            gates = dot(own_ref[1 + i], spread, ((0,), (0,)))
            mix_ref[i * rows : (i + 1) * rows] = jnp.where(hit, gates, 0.0).astype(bf16)

    both = dot(mix_ref[...], back_ref[...].reshape(slots, cols))
    mixed = both[:rows] + both[rows:]
    named = dot(own_ref[0], jnp.ones((experts, 128), bf16), ((0,), (0,)))
    moe = jnp.where(named[:, :1] > 0.5, mixed, cached_ref[...].astype(f32))
    merge, _, piece = attn_ref.shape
    for m in range(merge):
        here = slice(m * piece, (m + 1) * piece)
        hid = res_ref[:, here].astype(f32) + attn_ref[m].astype(f32)
        out_ref[:, here] = (hid + moe[:, here]).astype(bf16)


def combine(back, own, attn, residual, cached, span=2048):
    count, chips, cores, _, half = back.shape
    groups, rows, piece = attn.shape
    width = groups * piece
    experts = own.shape[1]
    merge = span // piece
    steps = half // span
    flat = pl.BlockSpec((rows, span), lambda j: (0, j))
    return pl.pallas_call(
        combine_kernel,
        grid=(width // span,),
        in_specs=[
            pl.BlockSpec(
                (count, chips, 1, SLOTS, span), lambda j: (0, 0, j // steps, 0, j % steps)
            ),
            pl.BlockSpec(own.shape, lambda j: (0, 0, 0)),
            pl.BlockSpec((merge, rows, piece), lambda j: (j, 0, 0)),
            flat,
            flat,
        ],
        out_specs=flat,
        out_shape=jax.ShapeDtypeStruct((rows, width), bf16),
        scratch_shapes=[pltpu.VMEM((2 * rows, experts * SLOTS), bf16)],
        compiler_params=params(30),
        name="combine",
    )(back, own, attn, residual, cached)


def exchange(blocks, axes):
    return lax.all_to_all(blocks, axes, split_axis=0, concat_axis=0, tiled=True)


def per_device(
    queries,
    keys,
    values,
    residual_in,
    cached_moe,
    norm_gain,
    still_masked,
    expert_ids,
    gate_weights,
    w_gate,
    w_up,
    w_down,
):
    rows, width = queries.shape[1:]
    seq_count = lax.axis_size("seq")
    exp_count = lax.axis_size("exp")
    devices = seq_count * exp_count
    experts = devices // 2
    cols = width // seq_count
    most = rows * 3 // 8
    all_axes = ("seq", "exp")
    gain = norm_gain[None, :]
    own_gain = lax.dynamic_slice_in_dim(gain, lax.axis_index("seq") * cols, cols, 1)
    weigh = 1.0 / jnp.square(norm_gain.astype(f32))
    high = weigh.astype(bf16)
    low = (weigh - high.astype(f32)).astype(bf16)
    weigh = jnp.pad(jnp.stack([high, low], axis=1), ((0, 0), (0, 126)))

    ring, cross, beside = [], [], []
    for s in range(seq_count):
        for p in range(exp_count):
            here = s * exp_count + p
            other_core = (s ^ 1) * exp_count + p
            other_chip = s * exp_count + (p ^ 1)
            both = (s ^ 1) * exp_count + (p ^ 1)
            if p % 2 == s % 2:
                ring.append((here, other_core))
                beside.append((here, other_core))
            else:
                ring.append((here, other_chip))
                cross.append((here, both))
    core = lax.axis_index("seq") % 2
    odd = lax.axis_index("exp") % 2
    role = jnp.stack([(core == odd).astype(jnp.int32), core.astype(jnp.int32)])

    first_down = take_half((1 - odd)[None].astype(jnp.int32), w_down[0])
    first_down = lax.ppermute(first_down, all_axes, ring)
    second_down = take_half(odd[None].astype(jnp.int32), w_down[0])
    second_down = lax.ppermute(second_down, all_axes, cross)
    pieces, own = prepare(
        queries[0],
        keys[0],
        values[0],
        residual_in[0],
        still_masked,
        expert_ids[0].T,
        gate_weights[0].T,
        seq_count,
        experts,
        most,
    )
    pieces = exchange(pieces, "seq")
    tied = lax.optimization_barrier((pieces, weigh, own_gain, first_down))
    pieces, weigh, own_gain, first_down = tied

    attn = attend(pieces, rows)
    sent = pick(attn, pieces, own_gain, experts)
    attn = exchange(attn, "seq")
    gate, sent = lax.optimization_barrier((w_gate[0], sent))
    gate, up = stage(gate, w_up[0])
    tied = lax.optimization_barrier((sent, attn, second_down, gate, up))
    sent, attn, second_down, gate, up = tied
    arrived = exchange(sent.reshape(devices, seq_count * SLOTS, cols), ("exp", "seq"))
    arrived = arrived.reshape(exp_count, seq_count, seq_count * SLOTS, cols)

    parts = 2
    per = seq_count * SLOTS // parts
    mine, first = [], []
    for part in range(parts):
        mine.append(expert_open(arrived, part, per, weigh, gate, up))
        arrived, mine[part] = lax.optimization_barrier((arrived, mine[part]))
        first.append(lax.ppermute(mine[part], all_axes, ring))
    first[0], mine[1] = lax.optimization_barrier((first[0], mine[1]))
    downs = (first_down, w_down[0], second_down)
    done = None
    for part in range(parts):
        second = lax.ppermute(first[part], all_axes, beside)
        acts = (first[part], mine[part], second)
        done = expert_close(role, acts, downs, part, seq_count, exp_count, done)
        if part == 0:
            first[1], done = lax.optimization_barrier((first[1], done))
    back = exchange(done.reshape(devices, SLOTS, width // 2), ("exp", "seq"))
    back = back.reshape(exp_count, seq_count // 2, 2, SLOTS, width // 2)
    out = combine(back, own, attn, residual_in[0], cached_moe[0])
    return out[None]


def solution(mesh):
    return jax.shard_map(
        per_device,
        mesh=mesh,
        in_specs=(
            P("exp", "seq", None),
            P("exp", "seq", None),
            P("exp", "seq", None),
            P("exp", "seq", None),
            P("exp", "seq", None),
            P(),
            P("exp", "seq"),
            P("exp", "seq", None),
            P("exp", "seq", None),
            P(("seq", "exp"), None, None),
            P(("seq", "exp"), None, None),
            P(("seq", "exp"), None, None),
        ),
        out_specs=P("exp", "seq", None),
        check_vma=False,
    )
```

```python
import functools
import math

import jax
import jax.numpy as jnp
from jax import lax
from jax.experimental import pallas as pl
from jax.experimental.pallas import tpu as pltpu
from jax.sharding import PartitionSpec as P

HEAD_DIM = 128
TOP = 8
SLOTS = 8
bf16 = jnp.bfloat16
f32 = jnp.float32


def params(mib):
    return pltpu.CompilerParams(vmem_limit_bytes=mib * 1024 * 1024)


def iota(shape, dim):
    return lax.broadcasted_iota(jnp.int32, shape, dim)


def ones(where):
    return jnp.where(where, jnp.float32(1.0), jnp.float32(0.0)).astype(bf16)


def dot(a, b, dims=((1,), (0,))):
    return lax.dot_general(a, b, (dims, ((), ())), preferred_element_type=f32)


def half_kernel(half_ref, down_ref, out_ref):
    del half_ref
    out_ref[...] = down_ref[...]


def take_half(half, down):
    depth, width = down.shape
    steps = 2
    span = width // 2 // steps
    return pl.pallas_call(
        half_kernel,
        grid_spec=pltpu.PrefetchScalarGridSpec(
            num_scalar_prefetch=1,
            grid=(steps,),
            in_specs=[pl.BlockSpec((depth, span), lambda c, half: (0, half[0] * steps + c))],
            out_specs=pl.BlockSpec((depth, span), lambda c, half: (0, c)),
        ),
        out_shape=jax.ShapeDtypeStruct((depth, width // 2), bf16),
        compiler_params=params(60),
        name="take_half",
    )(half, down)


def stage_kernel(gate_ref, up_ref, gate_out, up_out):
    gate_out[...] = gate_ref[...]
    up_out[...] = up_ref[...]


def stage(gate, up):
    width, depth = gate.shape
    steps = 8
    spec = pl.BlockSpec((width // steps, depth), lambda r: (r, 0))
    return pl.pallas_call(
        stage_kernel,
        grid=(steps,),
        in_specs=[spec, spec],
        out_specs=[spec, spec],
        out_shape=[
            jax.ShapeDtypeStruct(gate.shape, bf16),
            jax.ShapeDtypeStruct(up.shape, bf16),
        ],
        compiler_params=params(16),
        name="stage",
    )(gate, up)


def prepare_kernel(
    q_ref,
    k_ref,
    v_ref,
    res_ref,
    flag_ref,
    ids_ref,
    gates_ref,
    out_ref,
    own_ref,
    pick_ref,
    table_ref,
):
    rows = q_ref.shape[0]
    merge, _, cols = out_ref.shape
    experts, most = table_ref.shape
    extra = 3 * rows + most

    @pl.when(pl.program_id(0) == 0)
    def _():
        upper = ones(iota((rows, rows), 0) < iota((rows, rows), 1))
        masked = flag_ref[...] == 1
        rank = dot(ones(jnp.broadcast_to(flag_ref[...], (16, rows)) == 1), upper)[:1]
        pick = ones((iota((most, rows), 0).astype(f32) == rank) & masked)
        pick_ref[...] = pick
        slow = iota((experts, rows), 0)
        order = slow % TOP * TOP + slow // TOP
        named = jnp.zeros((experts, rows), f32)
        gates = jnp.zeros((experts, rows), f32)
        for k in range(TOP):
            hit = (order == ids_ref[k : k + 1, :]) & masked
            named = jnp.where(hit, 1.0, named)
            gates = jnp.where(hit, gates_ref[k : k + 1, :], gates)
        place = (named * (dot(named.astype(bf16), upper) + 1.0)).astype(bf16)
        high = gates.astype(bf16)
        own_ref[0] = place
        own_ref[1] = high
        own_ref[2] = (gates - high.astype(f32)).astype(bf16)
        table_ref[...] = dot(place, pick, ((1,), (1,))).astype(bf16)

    numbers = iota((16, rows), 1).astype(f32).astype(bf16)
    spot = dot(numbers, pick_ref[...], ((1,), (1,)))
    count = dot(jnp.ones((16, rows), bf16), pick_ref[...], ((1,), (1,)))
    spot = jnp.where(count > 0.5, spot, -1.0).astype(bf16)
    for m in range(merge):
        here = slice(m * cols, (m + 1) * cols)
        out_ref[m, :rows] = q_ref[:, here]
        out_ref[m, rows : 2 * rows] = k_ref[:, here]
        out_ref[m, 2 * rows : 3 * rows] = v_ref[:, here]
        out_ref[m, 3 * rows : extra] = dot(pick_ref[...], res_ref[:, here]).astype(bf16)
        out_ref[m, extra:] = jnp.zeros((16, cols), bf16)
        for h in range(experts // 16):
            out_ref[m, extra:, h * 128 : h * 128 + most] = table_ref[h * 16 : (h + 1) * 16]
            out_ref[m, extra:, h * 128 + 64 : h * 128 + 64 + most] = spot


def prepare(q, k, v, res, flags, ids, gates, groups, experts, most):
    rows, width = q.shape
    cols = width // groups
    total = 3 * rows + most + 16
    merge = 4
    piece = pl.BlockSpec((rows, merge * cols), lambda j: (0, j))
    return pl.pallas_call(
        prepare_kernel,
        grid=(groups // merge,),
        in_specs=[
            piece,
            piece,
            piece,
            piece,
            pl.BlockSpec((1, rows), lambda j: (0, 0)),
            pl.BlockSpec((TOP, rows), lambda j: (0, 0)),
            pl.BlockSpec((TOP, rows), lambda j: (0, 0)),
        ],
        out_specs=[
            pl.BlockSpec((merge, total, cols), lambda j: (j, 0, 0)),
            pl.BlockSpec((3, experts, rows), lambda j: (0, 0, 0)),
        ],
        out_shape=[
            jax.ShapeDtypeStruct((groups, total, cols), bf16),
            jax.ShapeDtypeStruct((3, experts, rows), bf16),
        ],
        scratch_shapes=[pltpu.VMEM((most, rows), bf16), pltpu.VMEM((experts, most), bf16)],
        compiler_params=params(60),
        name="prepare",
    )(q, k, v, res, flags, ids, gates)


def attend_kernel(in_ref, attn_ref, v_ref):
    blocks, rows, cols = attn_ref.shape
    length = blocks * rows
    scale = math.log2(math.e) / math.sqrt(HEAD_DIM)
    step = 2
    v_ref[:, HEAD_DIM:] = jnp.ones((length, HEAD_DIM), bf16)
    for h in range(cols // HEAD_DIM):
        here = slice(h * HEAD_DIM, (h + 1) * HEAD_DIM)
        k_all = in_ref[:, rows : 2 * rows, here].reshape(length, HEAD_DIM)
        v_ref[:, :HEAD_DIM] = in_ref[:, 2 * rows : 3 * rows, here].reshape(length, HEAD_DIM)
        for first in range(0, blocks, step):
            q_part = in_ref[first : first + step, :rows, here].reshape(step * rows, HEAD_DIM)
            scores = dot(q_part, k_all, ((1,), (1,)))
            peak = jnp.max(scores, axis=-1, keepdims=True)
            expo = jnp.exp2((scores - peak) * scale).astype(bf16)
            mixed = dot(expo, v_ref[...])
            attn = (mixed[:, :HEAD_DIM] / mixed[:, HEAD_DIM:]).astype(bf16)
            attn_ref[first : first + step, :, here] = attn.reshape(step, rows, HEAD_DIM)


def attend(pieces, rows, heads=2):
    blocks, _, cols = pieces.shape
    span = heads * HEAD_DIM
    return pl.pallas_call(
        attend_kernel,
        grid=(cols // span,),
        in_specs=[pl.BlockSpec((blocks, 3 * rows, span), lambda h: (0, 0, h))],
        out_specs=pl.BlockSpec((blocks, rows, span), lambda h: (0, 0, h)),
        out_shape=jax.ShapeDtypeStruct((blocks, rows, cols), bf16),
        scratch_shapes=[pltpu.VMEM((blocks * rows, 2 * HEAD_DIM), bf16)],
        compiler_params=params(60),
        name="attend",
    )(pieces)


def pick_kernel(attn_ref, res_ref, table_ref, gain_ref, out_ref, place_ref, spot_ref):
    blocks, rows, cols = attn_ref.shape
    experts, most = place_ref.shape[1] // SLOTS, place_ref.shape[2]

    @pl.when(pl.program_id(0) == 0)
    def _():
        wanted = iota((16, SLOTS, most), 1).astype(f32) + 1.0
        for b in range(blocks):
            for h in range(experts // 16):
                table = table_ref[b, :, h * 128 : h * 128 + most].astype(f32)
                hit = jnp.where(table[:, None, :] == wanted, 1.0, 0.0)
                place_ref[b, h * 128 : (h + 1) * 128] = hit.reshape(128, most).astype(bf16)
            spot = table_ref[b, :, 64 : 64 + most].astype(f32)[:1]
            spot_ref[b] = ones(iota((rows, most), 0).astype(f32) == spot)

    gain = gain_ref[...].astype(f32)
    for b in range(blocks):
        hidden = dot(spot_ref[b], attn_ref[b], ((0,), (0,))) + res_ref[b].astype(f32)
        sent = dot(place_ref[b], (hidden * gain).astype(bf16))
        sent = sent.reshape(TOP, experts // TOP, SLOTS, cols).astype(bf16)
        out_ref[:, 0, :, b] = sent
        out_ref[:, 1, :, b] = sent


def pick(attn, pieces, gain, experts):
    blocks, rows, cols = attn.shape
    total = pieces.shape[1]
    most = total - 3 * rows - 16
    span = 256
    blocked = experts // TOP
    return pl.pallas_call(
        pick_kernel,
        grid=(cols // span,),
        in_specs=[
            pl.BlockSpec((blocks, rows, span), lambda h: (0, 0, h)),
            pl.BlockSpec((blocks, most, span), lambda h: (0, 3 * rows // most, h)),
            pl.BlockSpec((blocks, 16, cols), lambda h: (0, total // 16 - 1, 0)),
            pl.BlockSpec((1, span), lambda h: (0, h)),
        ],
        out_specs=pl.BlockSpec(
            (TOP, 2, blocked, blocks, SLOTS, span), lambda h: (0, 0, 0, 0, 0, h)
        ),
        out_shape=jax.ShapeDtypeStruct((TOP, 2, blocked, blocks, SLOTS, cols), bf16),
        scratch_shapes=[
            pltpu.VMEM((blocks, experts * SLOTS, most), bf16),
            pltpu.VMEM((blocks, rows, most), bf16),
        ],
        compiler_params=params(60),
        name="pick",
    )(attn, pieces, pieces, gain)


def open_kernel(
    rows_ref, weigh_ref, gate_ref, up_ref, out_ref, gates_ref, ups_ref, square_ref
):
    step = pl.program_id(0)
    last = pl.num_programs(0) - 1
    count, merge, per, cols = rows_ref.shape
    total = count * per

    @pl.when(step == 0)
    def _():
        gates_ref[...] = jnp.zeros_like(gates_ref)
        ups_ref[...] = jnp.zeros_like(ups_ref)
        square_ref[...] = jnp.zeros_like(square_ref)

    tiles = max(total // 256, 1)
    tile = total // tiles
    for t in range(tiles):
        inside = slice(t * count // tiles, (t + 1) * count // tiles)
        rows = slice(t * tile, (t + 1) * tile)
        gate_part = gates_ref[rows]
        up_part = ups_ref[rows]
        square = square_ref[rows]
        for m in range(merge):
            here = slice(m * cols, (m + 1) * cols)
            x = rows_ref[inside, m].reshape(tile, cols)
            gate_part += dot(x, gate_ref[here])
            up_part += dot(x, up_ref[here])
            square += dot(x * x, weigh_ref[here])
        gates_ref[rows] = gate_part
        ups_ref[rows] = up_part
        square_ref[rows] = square

    @pl.when(step == last)
    def _():
        mean = (square_ref[:, :1] + square_ref[:, 1:2]) / ((last + 1) * merge * cols)
        scale = lax.rsqrt(mean + 1e-06)
        gate_full = gates_ref[...] * scale
        act = gate_full / (1.0 + jnp.exp(-gate_full)) * (ups_ref[...] * scale)
        out_ref[...] = act.astype(bf16)


def expert_open(arrived, part, per, weigh, gate, up):
    count, groups, _, cols = arrived.shape
    width, half = gate.shape
    total = count * per
    merge = 2
    weight = pl.BlockSpec((merge * cols, half), lambda n: (n, 0))
    return pl.pallas_call(
        open_kernel,
        grid=(groups // merge,),
        in_specs=[
            pl.BlockSpec((count, merge, per, cols), lambda n: (0, n, part, 0)),
            pl.BlockSpec((merge * cols, 128), lambda n: (n, 0)),
            weight,
            weight,
        ],
        out_specs=pl.BlockSpec((total, half), lambda n: (0, 0)),
        out_shape=jax.ShapeDtypeStruct((total, half), bf16),
        scratch_shapes=[
            pltpu.VMEM((total, half), f32),
            pltpu.VMEM((total, half), f32),
            pltpu.VMEM((total, 128), f32),
        ],
        compiler_params=params(26),
        cost_estimate=pl.CostEstimate(
            flops=4 * total * width * half,
            bytes_accessed=4 * width * half + 2 * total * (width + half),
            transcendentals=total * half,
        ),
        name="expert_open",
    )(arrived, weigh, gate, up)


def close_kernel(
    role_ref, first_ref, mine_ref, second_ref, first_down, own_down, second_down, *rest
):
    out_ref = rest[-1]
    def emit(act_ref, down_ref):
        result = dot(first_ref[...], first_down[...]) + dot(act_ref[...], down_ref[...])
        out_ref[...] = result.reshape(out_ref.shape).astype(bf16)

    @pl.when(role_ref[0] == 1)
    def _():
        emit(mine_ref, own_down)

    @pl.when(role_ref[0] == 0)
    def _():
        emit(second_ref, second_down)


def expert_close(role, acts, downs, part, groups, count, done):
    total, half = acts[0].shape
    width = downs[0].shape[1]
    span = 1024
    steps = width // span
    merge = total // (count * SLOTS)
    act = pl.BlockSpec((total, half), lambda c, role: (0, 0))
    held = [] if done is None else [done]

    def down(place):
        return pl.BlockSpec((half, span), lambda c, role: (0, place(c, role)))

    return pl.pallas_call(
        close_kernel,
        grid_spec=pltpu.PrefetchScalarGridSpec(
            num_scalar_prefetch=1,
            grid=(steps,),
            in_specs=[
                act,
                act,
                act,
                down(lambda c, role: c),
                down(lambda c, role: role[0] * (role[1] * steps + c)),
                down(lambda c, role: (1 - role[0]) * c),
            ]
            + [pl.BlockSpec(memory_space=pl.ANY)] * len(held),
            out_specs=pl.BlockSpec((count, merge, SLOTS, span), lambda c, role: (0, part, 0, c)),
        ),
        out_shape=jax.ShapeDtypeStruct((count, groups, SLOTS, width), bf16),
        input_output_aliases={7: 0} if held else {},
        compiler_params=params(44),
        cost_estimate=pl.CostEstimate(
            flops=4 * total * width * half,
            bytes_accessed=2 * (2 * width * half + total * (2 * half + width)),
            transcendentals=0,
        ),
        name="expert_close",
    )(role, *acts, *downs, *held)


def combine_kernel(back_ref, own_ref, attn_ref, res_ref, cached_ref, out_ref, mix_ref):
    _, experts, rows = own_ref.shape
    slots = experts * SLOTS
    cols = out_ref.shape[1]

    @pl.when(pl.program_id(0) == 0)
    def _():
        column = iota((experts, slots), 1) // SLOTS
        order = column // 8 * 8 + column % 4 * 2 + column // 4 % 2
        spread = ones(iota((experts, slots), 0) == order)
        slot = (iota((rows, slots), 1) % SLOTS + 1).astype(f32)
        hit = dot(own_ref[0], spread, ((0,), (0,))) == slot
        for i in range(2):
            gates = dot(own_ref[1 + i], spread, ((0,), (0,)))
            mix_ref[i * rows : (i + 1) * rows] = jnp.where(hit, gates, 0.0).astype(bf16)

    both = dot(mix_ref[...], back_ref[...].reshape(slots, cols))
    mixed = both[:rows] + both[rows:]
    named = dot(own_ref[0], jnp.ones((experts, 128), bf16), ((0,), (0,)))
    moe = jnp.where(named[:, :1] > 0.5, mixed, cached_ref[...].astype(f32))
    merge, _, piece = attn_ref.shape
    for m in range(merge):
        here = slice(m * piece, (m + 1) * piece)
        hid = res_ref[:, here].astype(f32) + attn_ref[m].astype(f32)
        out_ref[:, here] = (hid + moe[:, here]).astype(bf16)


def combine(back, own, attn, residual, cached, span=2048):
    count, chips, cores, _, half = back.shape
    groups, rows, piece = attn.shape
    width = groups * piece
    experts = own.shape[1]
    merge = span // piece
    steps = half // span
    flat = pl.BlockSpec((rows, span), lambda j: (0, j))
    return pl.pallas_call(
        combine_kernel,
        grid=(width // span,),
        in_specs=[
            pl.BlockSpec(
                (count, chips, 1, SLOTS, span), lambda j: (0, 0, j // steps, 0, j % steps)
            ),
            pl.BlockSpec(own.shape, lambda j: (0, 0, 0)),
            pl.BlockSpec((merge, rows, piece), lambda j: (j, 0, 0)),
            flat,
            flat,
        ],
        out_specs=flat,
        out_shape=jax.ShapeDtypeStruct((rows, width), bf16),
        scratch_shapes=[pltpu.VMEM((2 * rows, experts * SLOTS), bf16)],
        compiler_params=params(30),
        name="combine",
    )(back, own, attn, residual, cached)


def exchange(blocks, axes):
    return lax.all_to_all(blocks, axes, split_axis=0, concat_axis=0, tiled=True)


def per_device(
    queries,
    keys,
    values,
    residual_in,
    cached_moe,
    norm_gain,
    still_masked,
    expert_ids,
    gate_weights,
    w_gate,
    w_up,
    w_down,
):
    rows, width = queries.shape[1:]
    seq_count = lax.axis_size("seq")
    exp_count = lax.axis_size("exp")
    devices = seq_count * exp_count
    experts = devices // 2
    cols = width // seq_count
    most = rows * 3 // 8
    all_axes = ("seq", "exp")
    gain = norm_gain[None, :]
    own_gain = lax.dynamic_slice_in_dim(gain, lax.axis_index("seq") * cols, cols, 1)
    weigh = 1.0 / jnp.square(norm_gain.astype(f32))
    high = weigh.astype(bf16)
    low = (weigh - high.astype(f32)).astype(bf16)
    weigh = jnp.pad(jnp.stack([high, low], axis=1), ((0, 0), (0, 126)))

    ring, cross, beside = [], [], []
    for s in range(seq_count):
        for p in range(exp_count):
            here = s * exp_count + p
            other_core = (s ^ 1) * exp_count + p
            other_chip = s * exp_count + (p ^ 1)
            both = (s ^ 1) * exp_count + (p ^ 1)
            if p % 2 == s % 2:
                ring.append((here, other_core))
                beside.append((here, other_core))
            else:
                ring.append((here, other_chip))
                cross.append((here, both))
    core = lax.axis_index("seq") % 2
    odd = lax.axis_index("exp") % 2
    role = jnp.stack([(core == odd).astype(jnp.int32), core.astype(jnp.int32)])

    first_down = take_half((1 - odd)[None].astype(jnp.int32), w_down[0])
    first_down = lax.ppermute(first_down, all_axes, ring)
    second_down = take_half(odd[None].astype(jnp.int32), w_down[0])
    second_down = lax.ppermute(second_down, all_axes, cross)
    pieces, own = prepare(
        queries[0],
        keys[0],
        values[0],
        residual_in[0],
        still_masked,
        expert_ids[0].T,
        gate_weights[0].T,
        seq_count,
        experts,
        most,
    )
    pieces = exchange(pieces, "seq")
    tied = lax.optimization_barrier((pieces, weigh, own_gain, first_down))
    pieces, weigh, own_gain, first_down = tied

    attn = attend(pieces, rows)
    sent = pick(attn, pieces, own_gain, experts)
    attn = exchange(attn, "seq")
    gate, sent = lax.optimization_barrier((w_gate[0], sent))
    gate, up = stage(gate, w_up[0])
    tied = lax.optimization_barrier((sent, attn, second_down, gate, up))
    sent, attn, second_down, gate, up = tied
    arrived = exchange(sent.reshape(devices, seq_count * SLOTS, cols), ("exp", "seq"))
    arrived = arrived.reshape(exp_count, seq_count, seq_count * SLOTS, cols)

    parts = 2
    per = seq_count * SLOTS // parts
    mine, first = [], []
    for part in range(parts):
        mine.append(expert_open(arrived, part, per, weigh, gate, up))
        arrived, mine[part] = lax.optimization_barrier((arrived, mine[part]))
        first.append(lax.ppermute(mine[part], all_axes, ring))
    first[0], mine[1] = lax.optimization_barrier((first[0], mine[1]))
    downs = (first_down, w_down[0], second_down)
    done = None
    for part in range(parts):
        second = lax.ppermute(first[part], all_axes, beside)
        acts = (first[part], mine[part], second)
        done = expert_close(role, acts, downs, part, seq_count, exp_count, done)
        if part == 0:
            first[1], done = lax.optimization_barrier((first[1], done))
    back = exchange(done.reshape(devices, SLOTS, width // 2), ("exp", "seq"))
    back = back.reshape(exp_count, seq_count // 2, 2, SLOTS, width // 2)
    out = combine(back, own, attn, residual_in[0], cached_moe[0])
    return out[None]


def solution(mesh):
    return jax.shard_map(
        per_device,
        mesh=mesh,
        in_specs=(
            P("exp", "seq", None),
            P("exp", "seq", None),
            P("exp", "seq", None),
            P("exp", "seq", None),
            P("exp", "seq", None),
            P(),
            P("exp", "seq"),
            P("exp", "seq", None),
            P("exp", "seq", None),
            P(("seq", "exp"), None, None),
            P(("seq", "exp"), None, None),
            P(("seq", "exp"), None, None),
        ),
        out_specs=P("exp", "seq", None),
        check_vma=False,
    )
```
